512 devices in a mesh: dp: 4 (over x), expert: 8 (over y, core), shard: 16 (over z).
Axes of the slice: x: 4, y: 4, z: 16, core: 2. Of those that a mesh axis runs over, the one named last changes fastest.
Arguments:
- output_gradient: bfloat16 [65536, 3072], P(('dp', 'expert', 'shard')), may hold values from -24 to 24
- saved_router_scores: float32 [65536, 8], P(('dp', 'expert', 'shard')), may hold values from -8 to 8
- expert_choice_index: int32 [65536, 2], P(('dp', 'expert', 'shard')), may hold values from 0 to 7, as said below
- router_matrix: bfloat16 [8, 3072], replicated, may hold values from -0.109375 to 0.109375
- weight_normalized_entries: bfloat16 [3072, 8192], P('shard', 'expert'), may hold values from -1 to 1
- scales: bfloat16 [48, 8192], P('shard', 'expert'), may hold values from 0.0099487305 to 0.099609375
- stored_hidden_state: bfloat16 [4, 16, 256, 8192], P('dp', 'shard', None, 'expert'), may hold values from -6 to 6
- context: bfloat16 [65536, 3072], P(('dp', 'expert', 'shard')), may hold values from -6 to 6
- adapter_down_factor: bfloat16 [64, 3072], replicated, may hold values from -0.109375 to 0.109375
- adapter_up_factor: bfloat16 [64, 3072], replicated, may hold values from -0.109375 to 0.109375
Outputs:
- hidden_grad: bfloat16 [4, 16, 256, 8192], P('dp', 'shard', None, 'expert')
- token_grad: bfloat16 [65536, 3072], P(('dp', 'expert', 'shard'))
- grad_down: float32 [64, 3072], P(None, 'shard')
- up_factor_gradient: float32 [64, 3072], P(None, 'shard')
The draws below stay inside these ranges and needn't reach their ends.
Inputs may be any that keep to these rules, and one draw needn't show every extreme that they name: `expert_choice_index`: each token names two different experts and expert 0 at most once. The 128 tokens of one device block name expert 0 at most 32 times, and in every draw all device blocks of some pair of dp and shard indices name it exactly 32 times.
All inputs are finite; a program needn't handle non-finite values.
Results may differ from the reference program's by a relative error of at most 0.015.
Values may be sent and summed in bfloat16 or wider, within the bound.
A program may use at most 64 MiB of HBM per device.

```python
import math
import jax
import jax.numpy as jnp
from jax import lax

WINDOW_FEATURES = 3072
FF_WIN = 8192
ADAPTER_RANK = 64
BLOCK = 64
EXPERTS = 8
TOK_DEV = 128
CAP = 32
ROWS = 256
TOKENS = 65536
N_DP = 4
N_EXPERT = 8
N_SHARD = 16


def draw_expert_choice_index(key, part):
    blocks = TOKENS // TOK_DEV
    subkeys = jax.random.split(jax.random.fold_in(key, 11), 6)
    counts = jax.random.randint(subkeys[0], (blocks,), CAP // 2, CAP + 1)
    full_group = jax.random.randint(subkeys[1], (), 0, N_DP * N_SHARD)
    block_index = jnp.arange(blocks, dtype=jnp.int32)
    group_index = block_index // (N_EXPERT * N_SHARD) * N_SHARD + block_index % N_SHARD
    counts = jnp.where(group_index == full_group, CAP, counts)
    scores = jax.random.randint(subkeys[2], (blocks, TOK_DEV), 0, 65536) * TOK_DEV + jnp.arange(TOK_DEV, dtype=jnp.int32)[None, :]
    ranking = jnp.argsort(jnp.argsort(scores, axis=1), axis=1)
    in_window = (ranking < counts[:, None]).reshape(TOKENS)
    first_other = jax.random.randint(subkeys[3], (TOKENS,), 1, EXPERTS)
    step_other = jax.random.randint(subkeys[4], (TOKENS,), 1, EXPERTS - 1)
    second_other = 1 + (first_other - 1 + step_other) % (EXPERTS - 1)
    swap_side = jax.random.randint(subkeys[5], (TOKENS,), 0, 2) == 1
    zero_ids = jnp.zeros((TOKENS,), jnp.int32)
    column_first = jnp.where(in_window, jnp.where(swap_side, first_other, zero_ids), first_other)
    column_second = jnp.where(in_window, jnp.where(swap_side, zero_ids, first_other), second_other)
    return jnp.stack([column_first, column_second], axis=1).astype(jnp.int32)


def raised(drawn, stream_key, source, target, shards_of, factor):
    def block_of(position):
        return (jnp.arange(drawn.shape[position]) // (drawn.shape[position] // shards_of)).reshape((-1,) + (1,) * (drawn.ndim - 1 - position))

    near = jax.random.permutation(stream_key, shards_of)[block_of(target)]
    other_side = (block_of(target) + shards_of // 2) % shards_of
    return jnp.where((block_of(source) == near) | (block_of(source) == other_side), factor * drawn, drawn)


def block_levels(own_key, extent, cuts, low, top_value):
    level = 1.0
    for position, parts in cuts:
        steps = jax.random.uniform(jax.random.fold_in(jax.random.fold_in(own_key, 6), position), (parts,), jnp.float32, low / len(cuts), top_value / len(cuts))
        level = level * jnp.repeat(jnp.exp(steps), extent[position] // parts).reshape((-1,) + (1,) * (len(extent) - 1 - position))
    return level


def scatter_about(own_key, dims, width, limit, cuts=(), kind=jnp.bfloat16):
    values = width * jax.random.normal(own_key, dims, jnp.float32)
    if cuts:
        values = values * block_levels(own_key, dims, cuts, -0.22, 0.18)
    return jnp.clip(values, -limit, limit).astype(kind)


def noise_with(own_key, dims, deviation, reach, cuts, heavy, held_as=jnp.bfloat16):
    values = deviation * jax.random.normal(own_key, dims, jnp.float32)
    if cuts:
        values = values * block_levels(own_key, dims, cuts, -0.22, 0.18)
    return jnp.clip(raised(values, jax.random.fold_in(own_key, 3), *heavy), -reach, reach).astype(held_as)


def setup_inputs(seed: int = 0) -> dict:
    seeds = jax.random.split(jax.random.key(seed), 11)
    output_gradient = noise_with(seeds[0], (TOKENS, WINDOW_FEATURES), 1.0, 24.0, ((0, 512),), (0, 1, 512, 6.0))
    saved_router_scores = scatter_about(seeds[1], (TOKENS, EXPERTS), 2.0, 8.0, ((0, 512),), jnp.float32)
    expert_choice_index = draw_expert_choice_index(jax.random.fold_in(seeds[10], 71), 0)
    router_matrix = scatter_about(seeds[3], (EXPERTS, WINDOW_FEATURES), WINDOW_FEATURES ** -0.5, 0.109375)
    weight_normalized_entries = jnp.clip(jax.random.uniform(seeds[4], (WINDOW_FEATURES, FF_WIN), jnp.float32, -1.0, 1.0) * block_levels(seeds[4], (WINDOW_FEATURES, FF_WIN), ((0, 16), (1, 8)), -0.4, 0.0), -1.0, 1.0).astype(jnp.bfloat16)
    scales = jnp.clip(jnp.exp(math.log(0.099609375) - 2.3038113 * jax.random.uniform(seeds[5], (WINDOW_FEATURES // BLOCK, FF_WIN), jnp.float32) ** block_levels(seeds[5], (WINDOW_FEATURES // BLOCK, FF_WIN), ((0, 16), (1, 8)), -0.2, 0.2)), 0.0099487305, 0.099609375).astype(jnp.bfloat16)
    stored_hidden_state = scatter_about(seeds[6], (N_DP, N_SHARD, ROWS, FF_WIN), 1.0, 6.0, ((0, 4), (1, 16), (3, 8)))
    context = scatter_about(seeds[7], (TOKENS, WINDOW_FEATURES), 1.0, 6.0, ((0, 512),))
    adapter_down_factor = scatter_about(seeds[8], (ADAPTER_RANK, WINDOW_FEATURES), WINDOW_FEATURES ** -0.5, 0.109375)
    adapter_up_factor = scatter_about(seeds[9], (ADAPTER_RANK, WINDOW_FEATURES), WINDOW_FEATURES ** -0.5, 0.109375)
    return dict(output_gradient=output_gradient, saved_router_scores=saved_router_scores, expert_choice_index=expert_choice_index, router_matrix=router_matrix, weight_normalized_entries=weight_normalized_entries, scales=scales, stored_hidden_state=stored_hidden_state, context=context, adapter_down_factor=adapter_down_factor, adapter_up_factor=adapter_up_factor)


ADAPTER_SCALE = 0.25


def reference(output_gradient, saved_router_scores, expert_choice_index, router_matrix, weight_normalized_entries, scales, stored_hidden_state, context, adapter_down_factor, adapter_up_factor):
    labels = jnp.arange(EXPERTS, dtype=jnp.int32)
    choose = expert_choice_index[:, :, None] == labels[None, None, :]
    chosen = jnp.sum(jnp.where(choose, saved_router_scores[:, None, :], 0.0), axis=2)
    first_prob = 1.0 / (1.0 + jnp.exp(chosen[:, 1] - chosen[:, 0]))
    second_prob = 1.0 - first_prob
    in_window = expert_choice_index == 0
    window_flag = jnp.any(in_window, axis=1)
    blocks = TOKENS // TOK_DEV
    flag_int = window_flag.astype(jnp.int32).reshape(blocks, TOK_DEV)
    slot_index = (jnp.cumsum(flag_int, axis=1) - flag_int).reshape(TOKENS).astype(jnp.int32)
    block_of = (jnp.arange(TOKENS, dtype=jnp.int32) // TOK_DEV).astype(jnp.int32)
    route_probs = jnp.stack([first_prob, second_prob], axis=1).astype(jnp.bfloat16)
    window_prob = jnp.where(in_window[:, 0], route_probs[:, 0], route_probs[:, 1])
    target = jnp.where(window_flag, slot_index, CAP).astype(jnp.int32)
    buffer_rows = jnp.zeros((blocks, CAP, WINDOW_FEATURES), jnp.bfloat16).at[block_of, target].set(output_gradient, mode="drop")
    buffer_probs = jnp.zeros((blocks, CAP), jnp.bfloat16).at[block_of, target].set(window_prob, mode="drop")
    buffer_rows = buffer_rows.reshape(N_DP, N_EXPERT, N_SHARD, CAP, WINDOW_FEATURES).transpose(0, 2, 1, 3, 4).reshape(N_DP * N_SHARD, ROWS, WINDOW_FEATURES)
    buffer_probs = buffer_probs.reshape(N_DP, N_EXPERT, N_SHARD, CAP).transpose(0, 2, 1, 3).reshape(N_DP * N_SHARD, ROWS)
    weight = (weight_normalized_entries.astype(jnp.float32).reshape(WINDOW_FEATURES // BLOCK, BLOCK, FF_WIN) * scales.astype(jnp.float32)[:, None, :]).astype(jnp.bfloat16).reshape(WINDOW_FEATURES, FF_WIN)
    hidden_rows = stored_hidden_state.reshape(N_DP * N_SHARD, ROWS, FF_WIN)

    def one_group(group_item):
        rows_in, probs_in, hidden_in = group_item
        product = jnp.dot(rows_in, weight, preferred_element_type=jnp.float32)
        scaled_grads = (probs_in.astype(jnp.float32)[:, None] * product).astype(jnp.bfloat16)
        partial_value = jnp.sum(hidden_in.astype(jnp.float32) * product, axis=1)
        return scaled_grads, partial_value

    scaled_grads, prob_grad = lax.map(one_group, (buffer_rows, buffer_probs, hidden_rows))
    hidden_grad = scaled_grads.reshape(N_DP, N_SHARD, ROWS, FF_WIN)
    prob_grad = prob_grad.reshape(N_DP, N_SHARD, N_EXPERT, CAP)
    dp_index = block_of // (N_EXPERT * N_SHARD)
    source_expert = (block_of // N_SHARD) % N_EXPERT
    shard_index = block_of % N_SHARD
    window_grad = prob_grad[dp_index, shard_index, source_expert, jnp.minimum(slot_index, CAP - 1)]
    window_grad = jnp.where(window_flag, window_grad, 0.0)
    pair_grad = jnp.where(in_window, window_grad[:, None], 0.0)
    spread = first_prob * second_prob * (pair_grad[:, 0] - pair_grad[:, 1])
    sign_table = choose[:, 0, :].astype(jnp.float32) - choose[:, 1, :].astype(jnp.float32)
    logit_grad = (spread[:, None] * sign_table).astype(jnp.bfloat16)
    token_grad = jnp.dot(logit_grad, router_matrix, preferred_element_type=jnp.float32).astype(jnp.bfloat16)
    token_kept = lax.optimization_barrier(token_grad)
    residual_gradient = (output_gradient.astype(jnp.float32) + token_kept.astype(jnp.float32)).astype(jnp.bfloat16)
    narrow_input = lax.dot_general(context, adapter_down_factor, (((1,), (1,)), ((), ())), preferred_element_type=jnp.float32).astype(jnp.bfloat16)
    narrow_gradient = (ADAPTER_SCALE * lax.dot_general(residual_gradient, adapter_up_factor, (((1,), (1,)), ((), ())), preferred_element_type=jnp.float32)).astype(jnp.bfloat16)
    up_factor_gradient = ADAPTER_SCALE * lax.dot_general(narrow_input, residual_gradient, (((0,), (0,)), ((), ())), preferred_element_type=jnp.float32)
    grad_down = lax.dot_general(narrow_gradient, context, (((0,), (0,)), ((), ())), preferred_element_type=jnp.float32)
    return (hidden_grad, token_grad, grad_down, up_factor_gradient)
```

```python
import jax
import jax.numpy as jnp
from jax import lax
from jax.experimental import pallas as pl
from jax.experimental.pallas import tpu as pltpu
from jax.sharding import PartitionSpec as P

MESH = pl.DeviceIdType.MESH

ADAPTER_SCALE = 0.25


def reduce_kernel(
    a_ref, out_ref, twin_in, y_out, y_in, x_out, x_in, z_out, z_in, fin, send, recv
):
    d, e, s = lax.axis_index("dp"), lax.axis_index("expert"), lax.axis_index("shard")
    y, c = e // 2, e % 2
    flat = d * 8 + e

    barrier = pltpu.get_barrier_semaphore()
    for p in range(1, 32):
        q = (flat + p) % 32
        pl.semaphore_signal(barrier, inc=1, device_id=(q // 8, q % 8, s), device_id_type=MESH)
    for p in range(1, 16):
        pl.semaphore_signal(barrier, inc=1, device_id=(d, e, (s + p) % 16), device_id_type=MESH)
    pl.semaphore_wait(barrier, 46)

    def copy(src, dst, i, j, target):
        return pltpu.make_async_remote_copy(
            src_ref=src,
            dst_ref=dst,
            send_sem=send.at[i],
            recv_sem=recv.at[j],
            device_id=target,
            device_id_type=MESH,
        )

    half = a_ref.shape[1] // 2
    twin = (d, y * 2 + 1 - c, s)
    other = pl.ds(pl.multiple_of((1 - c) * half, half), half)
    mine = pl.ds(pl.multiple_of(c * half, half), half)
    first = copy(a_ref.at[:, other], twin_in, 0, 0, twin)
    first.start()
    first.wait()
    twin_in[...] += a_ref[:, mine]

    y_out[...] = twin_in[...].astype(jnp.bfloat16)
    sends = []
    for j in range(1, 4):
        to = (y + j) % 4
        sends.append(
            copy(
                y_out.at[pl.ds(pl.multiple_of(to * 32, 32), 32)],
                y_in.at[j - 1],
                j,
                j,
                (d, to * 2 + c, s),
            )
        )
    for one in sends:
        one.start()
    for one in sends:
        one.wait()
    x_out[...] = twin_in[pl.ds(pl.multiple_of(y * 32, 32), 32), :]
    for j in range(3):
        x_out[...] += y_in[j].astype(jnp.float32)

    sends = []
    for j in range(1, 4):
        to = (d + j) % 4
        sends.append(
            copy(
                x_out.at[pl.ds(pl.multiple_of(to * 8, 8), 8)],
                x_in.at[j - 1],
                3 + j,
                3 + j,
                (to, e, s),
            )
        )
    for one in sends:
        one.start()
    for one in sends:
        one.wait()
    part = x_out[pl.ds(pl.multiple_of(d * 8, 8), 8), :] + x_in[0] + x_in[1] + x_in[2]

    for j in range(8):
        z_out[j, :, 0:192] = part[:, 192 * j : 192 * j + 192]
    z_out[:, :, 192:256] = jnp.zeros((8, 8, 64), jnp.float32)
    keeps = s // 8 == c
    for j in range(8):
        k = c * 8 + j

        @pl.when(k != s)
        def _():
            copy(z_out.at[j], z_in.at[s], 7 + j, 7 + s, (d, e, k)).start()

    @pl.when(keeps)
    def _():
        z_in[s] = z_out[s % 8]
        for i in range(16):

            @pl.when(i != s)
            def _():
                copy(z_out.at[0], z_in.at[i], 7, 7 + i, (d, e, (s + 1) % 16)).wait_recv()

        total = z_in[0]
        for i in range(1, 16):
            total = total + z_in[i]
        fin[y * 4 + d] = total
        for p in range(1, 32):
            q = (flat + p) % 32
            slot = y * 4 + d
            copy(
                fin.at[slot], fin.at[slot], 14 + p, 23 + slot, (q // 8, q % 8, s)
            ).start()

    for t in range(16):

        @pl.when((t != y * 4 + d) | jnp.logical_not(keeps))
        def _():
            copy(fin.at[t], fin.at[t], 0, 23 + t, twin).wait_recv()

    for j in range(8):

        @pl.when(c * 8 + j != s)
        def _():
            copy(z_out.at[j], z_in.at[j], 7 + j, 7, twin).wait_send()

    @pl.when(keeps)
    def _():
        for p in range(1, 32):
            copy(fin.at[0], fin.at[0], 14 + p, 23, twin).wait_send()

    for t in range(16):
        out_ref[8 * t : 8 * t + 8, :] = fin[t, :, 0:192]


def reduce_all(stacked):
    f32 = jnp.float32
    return pl.pallas_call(
        reduce_kernel,
        out_shape=jax.ShapeDtypeStruct((128, 192), f32),
        in_specs=[pl.BlockSpec(memory_space=pltpu.VMEM)],
        out_specs=pl.BlockSpec(memory_space=pltpu.VMEM),
        scratch_shapes=[
            pltpu.VMEM((128, 1536), f32),
            pltpu.VMEM((128, 1536), jnp.bfloat16),
            pltpu.VMEM((3, 32, 1536), jnp.bfloat16),
            pltpu.VMEM((32, 1536), f32),
            pltpu.VMEM((3, 8, 1536), f32),
            pltpu.VMEM((8, 8, 256), f32),
            pltpu.VMEM((16, 8, 256), f32),
            pltpu.VMEM((16, 8, 256), f32),
            pltpu.SemaphoreType.DMA((46,)),
            pltpu.SemaphoreType.DMA((39,)),
        ],
        compiler_params=pltpu.CompilerParams(
            collective_id=0, has_side_effects=True, vmem_limit_bytes=32 << 20
        ),
    )(stacked)


def per_device(
    output_gradient,
    saved_router_scores,
    expert_choice_index,
    router_matrix,
    weight_normalized_entries,
    scales,
    stored_hidden_state,
    context,
    adapter_down_factor,
    adapter_up_factor,
):
    expert_count = lax.axis_size("expert")
    tokens = output_gradient.shape[0]
    experts = saved_router_scores.shape[1]
    row_count = stored_hidden_state.shape[2]
    capacity = row_count // expert_count
    ff_share = stored_hidden_state.shape[3]
    block_size = weight_normalized_entries.shape[0] // scales.shape[0]
    labels = jnp.arange(experts, dtype=jnp.int32)
    choose = expert_choice_index[:, :, None] == labels[None, None, :]
    chosen = jnp.sum(jnp.where(choose, saved_router_scores[:, None, :], 0.0), axis=2)
    first_prob = 1.0 / (1.0 + jnp.exp(chosen[:, 1] - chosen[:, 0]))
    second_prob = 1.0 - first_prob
    in_window = expert_choice_index == 0
    window_flag = jnp.any(in_window, axis=1)
    flag_int = window_flag.astype(jnp.int32)
    positions = jnp.arange(tokens, dtype=jnp.int32)
    slot_index = jnp.sum(
        jnp.where(positions[None, :] < positions[:, None], flag_int[None, :], 0), axis=1
    )
    route_probs = jnp.stack([first_prob, second_prob], axis=1).astype(jnp.bfloat16)
    window_prob = jnp.where(in_window[:, 0], route_probs[:, 0], route_probs[:, 1])
    slot_labels = jnp.arange(capacity, dtype=jnp.int32)
    placement = (window_flag[None, :] & (slot_index[None, :] == slot_labels[:, None])).astype(
        jnp.bfloat16
    )
    send_rows = jnp.dot(placement, output_gradient, preferred_element_type=jnp.float32).astype(
        jnp.bfloat16
    )
    send_probs = jnp.dot(placement, window_prob, preferred_element_type=jnp.float32).astype(
        jnp.bfloat16
    )
    all_rows, all_probs = (
        lax.all_gather(send_rows, "expert", axis=0, tiled=True),
        lax.all_gather(send_probs, "expert", axis=0, tiled=True),
    )
    code_blocks = weight_normalized_entries.reshape(scales.shape[0], block_size, ff_share)
    own_weight = (
        (code_blocks.astype(jnp.float32) * scales.astype(jnp.float32)[:, None, :])
        .astype(jnp.bfloat16)
        .reshape(weight_normalized_entries.shape[0], ff_share)
    )
    product = jnp.dot(
        all_rows,
        lax.all_gather(own_weight, "shard", axis=0, tiled=True),
        preferred_element_type=jnp.float32,
    )
    hidden_grad = (all_probs.astype(jnp.float32)[:, None] * product).astype(jnp.bfloat16)
    partial_value = jnp.sum(stored_hidden_state[0, 0].astype(jnp.float32) * product, axis=1)
    returned = lax.psum_scatter(partial_value, "expert", scatter_dimension=0, tiled=True)
    window_grad = jnp.where(window_flag, returned[jnp.minimum(slot_index, capacity - 1)], 0.0)
    pair_grad = jnp.where(in_window, window_grad[:, None], 0.0)
    spread = first_prob * second_prob * (pair_grad[:, 0] - pair_grad[:, 1])
    sign_table = choose[:, 0, :].astype(jnp.float32) - choose[:, 1, :].astype(jnp.float32)
    logit_grad = (spread[:, None] * sign_table).astype(jnp.bfloat16)
    token_grad = jnp.dot(logit_grad, router_matrix, preferred_element_type=jnp.float32).astype(
        jnp.bfloat16
    )
    token_kept = lax.optimization_barrier(token_grad)
    residual_gradient = (
        output_gradient.astype(jnp.float32) + token_kept.astype(jnp.float32)
    ).astype(jnp.bfloat16)
    narrow_input = lax.dot_general(
        context, adapter_down_factor, (((1,), (1,)), ((), ())), preferred_element_type=jnp.float32
    ).astype(jnp.bfloat16)
    narrow_gradient = (
        ADAPTER_SCALE
        * lax.dot_general(
            residual_gradient,
            adapter_up_factor,
            (((1,), (1,)), ((), ())),
            preferred_element_type=jnp.float32,
        )
    ).astype(jnp.bfloat16)
    partial_up_gradient = ADAPTER_SCALE * lax.dot_general(
        narrow_input,
        residual_gradient,
        (((0,), (0,)), ((), ())),
        preferred_element_type=jnp.float32,
    )
    part_down = lax.dot_general(
        narrow_gradient, context, (((0,), (0,)), ((), ())), preferred_element_type=jnp.float32
    )
    summed = reduce_all(jnp.concatenate([partial_up_gradient, part_down], axis=0))
    up_factor_gradient = summed[:64]
    grad_down = summed[64:]
    return (
        hidden_grad.reshape(stored_hidden_state.shape),
        token_grad,
        grad_down,
        up_factor_gradient,
    )


def solution(mesh):
    in_specs = (
        P(("dp", "expert", "shard"), None),
        P(("dp", "expert", "shard"), None),
        P(("dp", "expert", "shard"), None),
        P(),
        P("shard", "expert"),
        P("shard", "expert"),
        P("dp", "shard", None, "expert"),
        P(("dp", "expert", "shard"), None),
        P(),
        P(),
    )
    out_specs = (
        P("dp", "shard", None, "expert"),
        P(("dp", "expert", "shard"), None),
        P(None, "shard"),
        P(None, "shard"),
    )
    return jax.shard_map(
        per_device, mesh=mesh, in_specs=in_specs, out_specs=out_specs, check_vma=False
    )
```

```python
import jax
import jax.numpy as jnp
from jax import lax
from jax.experimental import pallas as pl
from jax.experimental.pallas import tpu as pltpu
from jax.sharding import PartitionSpec as P

ADAPTER_SCALE = 0.25
MESH = pl.DeviceIdType.MESH
F32, BF16 = jnp.float32, jnp.bfloat16
FEATURES, TAIL, SLOTS, RANK = 3072, 128, 32, 64
SENDS, RECVS = 110, 130


def dot(a, b, over, precision=None):
    return lax.dot_general(
        a, b, ((over[:1], over[1:]), ((), ())), precision=precision, preferred_element_type=F32
    )


def layer_kernel(
    og,
    scores,
    idx,
    router,
    codes,
    scales,
    stored,
    ctx,
    down,
    up,
    hidden_out,
    token_out,
    up_out,
    down_out,
    rows,
    weight,
    prod_out,
    prod_in,
    hidden,
    token,
    pg_out,
    pg_in,
    adapt,
    a_twin,
    a_y_out,
    a_y_in,
    a_x_out,
    a_x_in,
    a_z_out,
    a_z_in,
    b_pad,
    b_twin,
    b_z_out,
    b_z_in,
    y_gather,
    x_gather,
    router_pad,
    send,
    recv,
    local,
):
    d, e, s = lax.axis_index("dp"), lax.axis_index("expert"), lax.axis_index("shard")
    y, c = e // 2, e % 2
    twin = (d, y * 2 + 1 - c, s)
    keeps = s // 8 == c

    barrier = pltpu.get_barrier_semaphore()
    for target in (
        twin,
        ((d + 1) % 4, e, s),
        ((d + 3) % 4, e, s),
        (d, (e + 2) % 8, s),
        (d, (e + 6) % 8, s),
        (d, e, (s + 1) % 16),
        (d, e, (s + 15) % 16),
    ):
        pl.semaphore_signal(barrier, inc=1, device_id=target, device_id_type=MESH)

    made = []
    used = [0, 0]

    def describe(src, dst, i, j, target):
        return pltpu.make_async_remote_copy(
            src_ref=src,
            dst_ref=dst,
            send_sem=send.at[i],
            recv_sem=recv.at[j],
            device_id=target,
            device_id_type=MESH,
        )

    def start(src, dst, target):
        one = describe(src, dst, used[0], used[1], target)
        used[0] += 1
        used[1] += 1
        one.start()
        made.append(one)
        return one

    def row_range(first, count, step):
        return pl.ds(pl.multiple_of(first, step), count)

    quarter = pl.ds(pl.multiple_of(d * 256, 256), 256)
    factors = scales[:, quarter].astype(F32)
    for k in range(3):
        block = codes[64 * k : 64 * k + 64, quarter].astype(F32) * factors[k : k + 1, :]
        weight[row_range(s * 192 + 64 * k, 64, 64), :] = block.astype(BF16)

    labels = lax.broadcasted_iota(jnp.int32, (128, 8), 1)
    first_choice, second_choice = idx[:, 0:1], idx[:, 1:2]
    choose_first, choose_second = labels == first_choice, labels == second_choice
    score = scores[...]
    chosen_first = jnp.sum(jnp.where(choose_first, score, 0.0), axis=1, keepdims=True)
    chosen_second = jnp.sum(jnp.where(choose_second, score, 0.0), axis=1, keepdims=True)
    first_prob = 1.0 / (1.0 + jnp.exp(chosen_second - chosen_first))
    second_prob = 1.0 - first_prob
    in_first = (first_choice == 0).astype(F32)
    in_second = (second_choice == 0).astype(F32)
    flag = in_first + in_second
    before = lax.broadcasted_iota(jnp.int32, (128, 128), 0) > lax.broadcasted_iota(
        jnp.int32, (128, 128), 1
    )
    slot = dot(
        before.astype(BF16), jnp.broadcast_to(flag, (128, 128)).astype(BF16), (1, 0)
    )
    slot_labels = lax.broadcasted_iota(jnp.int32, (128, SLOTS), 1).astype(F32)
    placement = jnp.where(slot[:, 0:SLOTS] == slot_labels, jnp.broadcast_to(flag, (128, SLOTS)), 0.0)
    window_prob = jnp.where(in_first > 0.0, first_prob, second_prob).astype(BF16)
    placed = placement.astype(BF16)

    f = d * (1 - c) + y * c
    g = y * (1 - c) + d * c

    def at_fg(ff, gg):
        return (ff * (1 - c) + gg * c, gg * (1 - c) + ff * c)

    def device_fg(ff, gg):
        dd, yy = at_fg(ff % 4, gg % 4)
        return (dd, yy * 2 + c, s)

    def slot_fg(ff, gg):
        dd, yy = at_fg(ff % 4, gg % 4)
        return (dd * 8 + yy * 2 + c) * SLOTS

    own = row_range(slot_fg(f, g), SLOTS, SLOTS)
    rows[own, 0:FEATURES] = dot(placed, og[...], (0, 0)).astype(BF16)
    rows[own, FEATURES : FEATURES + TAIL] = dot(
        placed, jnp.broadcast_to(window_prob.astype(F32), (128, TAIL)).astype(BF16), (0, 0)
    ).astype(BF16)

    pl.semaphore_wait(barrier, 7)

    f_plus, f_minus = device_fg(f + 1, g), device_fg(f + 3, g)
    g_plus, g_minus = device_fg(f, g + 1), device_fg(f, g + 3)
    z_plus, z_minus = (d, e, (s + 1) % 16), (d, e, (s + 15) % 16)

    def pass_rows(ff, gg, target, part=None):
        first, count = slot_fg(ff, gg), SLOTS
        if part is not None:
            first, count = first + 16 * part, 16
        piece = rows.at[row_range(first, count, 16)]
        return start(piece, piece, target)

    def pass_weight(owner, part, target):
        piece = weight.at[row_range((owner % 16) * 192 + 96 * part, 96, 16)]
        return start(piece, piece, target)

    z_up = [[None, None] for _ in range(8)]
    z_down = [[None, None] for _ in range(8)]
    for part in range(2):
        z_up[0][part] = pass_weight(s, part, z_plus)
        z_down[0][part] = pass_weight(s, part, z_minus)
    to_f_plus = pass_rows(f, g, f_plus)
    to_f_minus = pass_rows(f, g, f_minus)
    g_up, g_down, g_up_half, g_down_half = [], [], [], []
    to_twin = []

    def spread_g(ff):
        g_up.append(pass_rows(ff, g, g_plus))
        g_down.append(pass_rows(ff, g, g_minus))
        to_twin.append(pass_rows(ff, g, twin))

    spread_g(f)

    low_in = dot(ctx[...], down[...], (1, 1)).astype(BF16)
    low_grad = (ADAPTER_SCALE * dot(og[...], up[...], (1, 1))).astype(BF16)
    adapt[0:RANK, :] = dot(low_in, og[...], (0, 0))
    adapt[RANK : 2 * RANK, :] = dot(low_grad, ctx[...], (0, 0))
    half = FEATURES // 2
    to_twin_a = start(
        adapt.at[:, pl.ds(pl.multiple_of((1 - c) * half, half), half)], a_twin, twin
    )

    def ring_step(h):
        for part in range(2):
            for chain, turn, target in ((z_up, -1, z_plus), (z_down, 1, z_minus)):
                if chain[h][part] is None:
                    continue
                chain[h][part].wait_recv()
                further = h + 1 < 7 or (h + 1 == 7 and part == (0 if chain is z_up else 1))
                if further:
                    chain[h + 1][part] = pass_weight(s + 16 + turn * (h + 1), part, target)

    from_f = (f, f + 3, f + 1, f + 2)

    def take_g(i):
        g_up[i].wait_recv()
        g_up_half.append(pass_rows(from_f[i], g + 3, g_plus, 0))
        g_down[i].wait_recv()
        g_down_half.append(pass_rows(from_f[i], g + 1, g_minus, 1))
        to_twin.append(pass_rows(from_f[i], g + 3, twin))
        to_twin.append(pass_rows(from_f[i], g + 1, twin))

    def take_g_half(i):
        g_up_half[i].wait_recv()
        g_down_half[i].wait_recv()
        to_twin.append(pass_rows(from_f[i], g + 2, twin))

    ring_step(0)
    to_f_plus.wait_recv()
    f_up_half = pass_rows(f + 3, g, f_plus, 0)
    spread_g(f + 3)
    to_f_minus.wait_recv()
    f_down_half = pass_rows(f + 1, g, f_minus, 1)
    spread_g(f + 1)
    ring_step(1)
    take_g(0)
    f_up_half.wait_recv()
    f_down_half.wait_recv()
    spread_g(f + 2)
    ring_step(2)
    take_g_half(0)
    ring_step(3)
    take_g(1)
    ring_step(4)
    take_g(2)
    take_g_half(1)
    ring_step(5)

    to_twin_a.wait_recv()
    a_twin[...] += adapt[:, pl.ds(pl.multiple_of(c * half, half), half)]
    a_y_out[...] = a_twin[...].astype(BF16)

    take_g(3)
    take_g_half(2)
    ring_step(6)
    take_g_half(3)
    a_y = []
    for j in range(1, 4):
        to = (y + j) % 4
        a_y.append(
            start(a_y_out.at[row_range(to * 32, 32, 32)], a_y_in.at[j - 1], (d, to * 2 + c, s))
        )
    for k in range(16):
        router_pad[k] = router[:, 192 * k : 192 * k + 192].astype(F32)
    up_router = dot(up[...], router[...], (1, 1))
    ring_step(7)
    for one in to_twin:
        one.wait_recv()

    exchange = []
    for j in (2, 1, 3, 0):
        to = (d + j) % 4
        product = dot(
            rows[row_range(to * 256, 256, 256), 0:FEATURES], weight[...], (1, 0)
        ).astype(BF16)
        if j == 0:
            prod_in[d] = product
        else:
            prod_out[to] = product
            exchange.append((j, start(prod_out.at[to], prod_in.at[d], (to, e, s))))

    for one in a_y:
        one.wait_recv()
    a_x_out[...] = a_twin[row_range(y * 32, 32, 32), :]
    for j in range(3):
        a_x_out[...] += a_y_in[j].astype(F32)
    a_x = []
    for j in range(1, 4):
        to = (d + j) % 4
        a_x.append(start(a_x_out.at[row_range(to * 8, 8, 8)], a_x_in.at[j - 1], (to, e, s)))

    own_probs = rows[row_range(d * 256, 256, 256), FEATURES : FEATURES + TAIL].astype(F32)

    def take_product(q, first):
        total = None
        for k in range(2):
            columns = pl.ds(pl.multiple_of(q * 256 + 128 * k, 128), 128)
            piece = prod_in[q, :, 128 * k : 128 * k + 128].astype(F32)
            hidden[:, columns] = (own_probs * piece).astype(BF16)
            term = stored[:, columns].astype(F32) * piece
            total = term if total is None else total + term
        if first:
            pg_out[...] = total
        else:
            pg_out[...] += total

    take_product(d, True)
    for j, one in exchange[1:] + exchange[:1]:
        one.wait_recv()
        take_product((d + 4 - j) % 4, False)
    hidden_copy = pltpu.make_async_copy(hidden, hidden_out, local.at[0])
    hidden_copy.start()

    pg = []
    for p in (4, 5, 3, 2, 6, 7, 1):
        to = (e + p) % 8
        pg.append(start(pg_out.at[row_range(to * 32, 32, 32)], pg_in.at[e], (d, to, s)))
    pg_in[e] = pg_out[row_range(e * 32, 32, 32), :]

    for one in a_x:
        one.wait_recv()
    part = a_x_out[row_range(d * 8, 8, 8), :] + a_x_in[0] + a_x_in[1] + a_x_in[2]
    for j in range(8):
        a_z_out[j, :, 0:192] = part[:, 192 * j : 192 * j + 192]
    a_z_out[:, :, 192:256] = jnp.zeros((8, 8, 64), F32)

    def over_z(out, landing):
        first_send, first_recv = used
        used[0] += 8
        used[1] += 16
        for j in range(8):
            k = c * 8 + j

            @pl.when(k != s)
            def _():
                describe(
                    out.at[j], landing.at[s], first_send + j, first_recv + s, (d, e, k)
                ).start()

        return first_send, first_recv

    def sum_over_z(out, landing, first):
        landing[s] = out[s % 8]
        for i in range(16):

            @pl.when(i != s)
            def _():
                describe(out.at[0], landing.at[i], first[0], first[1] + i, z_plus).wait_recv()

        total = landing[0]
        for i in range(1, 16):
            total = total + landing[i]
        return total

    def sent_over_z(out, first):
        for j in range(8):

            @pl.when(c * 8 + j != s)
            def _():
                describe(out.at[j], out.at[j], first[0] + j, first[1], z_plus).wait_send()

    first_a = over_z(a_z_out, a_z_in)

    for one in pg:
        one.wait_recv()
    returned = pg_in[0]
    for k in range(1, 8):
        returned = returned + pg_in[k]
    window_grad = jnp.sum(
        dot(placement, returned, (1, 0), lax.Precision.HIGHEST), axis=1, keepdims=True
    )
    spread = first_prob * second_prob * (window_grad * in_first - window_grad * in_second)
    sign = choose_first.astype(F32) - choose_second.astype(F32)
    logit_grad = (spread * sign).astype(BF16)

    by_feature = dot(logit_grad, ctx[...], (0, 0))
    by_rank = dot(logit_grad, low_in, (0, 0))
    for k in range(16):
        b_pad[k, :, 0:192] = by_feature[:, 192 * k : 192 * k + 192]
        b_pad[k, :, 192:256] = by_rank
    to_twin_b = start(b_pad.at[row_range((1 - c) * 8, 8, 8)], b_twin, twin)
    token[...] = dot(logit_grad, router[...], (1, 0)).astype(BF16)
    token_copy = pltpu.make_async_copy(token, token_out, local.at[1])
    token_copy.start()
    to_twin_b.wait_recv()
    b_z_out[...] = b_pad[row_range(c * 8, 8, 8)] + b_twin[...]
    first_b = over_z(b_z_out, b_z_in)

    first_y = list(used)
    first_x = [used[0] + 3, used[1] + 3]
    last = [used[0] + 6, used[1] + 6]

    @pl.when(keeps)
    def _():
        y_gather[y, 0:8, :] = sum_over_z(a_z_out, a_z_in, first_a)
        y_gather[y, 8:16, :] = sum_over_z(b_z_out, b_z_in, first_b)
        copies = []
        for j in range(1, 4):
            copies.append(
                describe(
                    y_gather.at[y],
                    y_gather.at[y],
                    first_y[0] + j - 1,
                    first_y[1] + j - 1,
                    (d, ((y + j) % 4) * 2 + c, s),
                )
            )
        for one in copies:
            one.start()
        for one in copies:
            one.wait_recv()
        for k in range(4):
            x_gather[d, 8 * k : 8 * k + 8, :] = y_gather[k, 0:8, :]
        x_gather[d, 32:40, :] = (
            y_gather[0, 8:16, :] + y_gather[1, 8:16, :] + y_gather[2, 8:16, :] + y_gather[3, 8:16, :]
        )
        for j in range(1, 4):
            copies.append(
                describe(
                    x_gather.at[d],
                    x_gather.at[d],
                    first_x[0] + j - 1,
                    first_x[1] + j - 1,
                    ((d + j) % 4, e, s),
                )
            )
        for one in copies[3:]:
            one.start()
        for one in copies[3:]:
            one.wait_recv()
        across = describe(x_gather, x_gather, last[0], last[1], twin)
        across.start()
        across.wait_send()
        for one in copies:
            one.wait_send()

    @pl.when(jnp.logical_not(keeps))
    def _():
        describe(x_gather, x_gather, last[0], last[1], twin).wait_recv()

    total = (
        x_gather[0, 32:40, :] + x_gather[1, 32:40, :] + x_gather[2, 32:40, :] + x_gather[3, 32:40, :]
    )
    exact = lax.Precision.HIGHEST
    more_up = dot(total[:, 192:256], router_pad[s], (0, 0), exact)
    more_down = dot(up_router, total[:, 0:192], (1, 0), exact)
    for k in range(4):
        for j in range(4):
            first = 32 * k + 8 * j
            block = x_gather[j, 8 * k : 8 * k + 8, 0:192]
            if k < 2:
                up_out[first : first + 8, :] = ADAPTER_SCALE * (block + more_up[first : first + 8])
            else:
                first = first - RANK
                down_out[first : first + 8, :] = block + ADAPTER_SCALE * more_down[first : first + 8]

    sent_over_z(a_z_out, first_a)
    sent_over_z(b_z_out, first_b)
    for one in made:
        one.wait_send()
    hidden_copy.wait()
    token_copy.wait()


def per_device(og, scores, idx, router, codes, scales, stored, ctx, down, up):
    vmem = pl.BlockSpec(memory_space=pltpu.VMEM)
    anywhere = pl.BlockSpec(memory_space=pl.ANY)
    shape = jax.ShapeDtypeStruct
    hidden_grad, token_grad, up_gradient, grad_down = pl.pallas_call(
        layer_kernel,
        out_shape=(
            shape((256, 1024), BF16),
            shape((128, FEATURES), BF16),
            shape((RANK, 192), F32),
            shape((RANK, 192), F32),
        ),
        in_specs=[vmem] * 10,
        out_specs=(anywhere, anywhere, vmem, vmem),
        scratch_shapes=[
            pltpu.VMEM((1024, FEATURES + TAIL), BF16),
            pltpu.VMEM((FEATURES, 256), BF16),
            pltpu.VMEM((4, 256, 256), BF16),
            pltpu.VMEM((4, 256, 256), BF16),
            pltpu.VMEM((256, 1024), BF16),
            pltpu.VMEM((128, FEATURES), BF16),
            pltpu.VMEM((256, 128), F32),
            pltpu.VMEM((8, 32, 128), F32),
            pltpu.VMEM((128, FEATURES), F32),
            pltpu.VMEM((128, FEATURES // 2), F32),
            pltpu.VMEM((128, FEATURES // 2), BF16),
            pltpu.VMEM((3, 32, FEATURES // 2), BF16),
            pltpu.VMEM((32, FEATURES // 2), F32),
            pltpu.VMEM((3, 8, FEATURES // 2), F32),
            pltpu.VMEM((8, 8, 256), F32),
            pltpu.VMEM((16, 8, 256), F32),
            pltpu.VMEM((16, 8, 256), F32),
            pltpu.VMEM((8, 8, 256), F32),
            pltpu.VMEM((8, 8, 256), F32),
            pltpu.VMEM((16, 8, 256), F32),
            pltpu.VMEM((4, 16, 256), F32),
            pltpu.VMEM((4, 40, 256), F32),
            pltpu.VMEM((16, 8, 192), F32),
            pltpu.SemaphoreType.DMA((SENDS,)),
            pltpu.SemaphoreType.DMA((RECVS,)),
            pltpu.SemaphoreType.DMA((2,)),
        ],
        compiler_params=pltpu.CompilerParams(
            collective_id=0, has_side_effects=True, vmem_limit_bytes=48 << 20
        ),
    )(og, scores, idx, router, codes, scales, stored[0, 0], ctx, down, up)
    return hidden_grad.reshape(stored.shape), token_grad, grad_down, up_gradient


def solution(mesh):
    tokens = P(("dp", "expert", "shard"), None)
    blocks = P("shard", "expert")
    hidden = P("dp", "shard", None, "expert")
    shares = P(None, "shard")
    return jax.shard_map(
        per_device,
        mesh=mesh,
        in_specs=(tokens, tokens, tokens, P(), blocks, blocks, hidden, tokens, P(), P()),
        out_specs=(hidden, tokens, shares, shares),
        check_vma=False,
    )
```

```python
import jax
import jax.numpy as jnp
from jax import lax
from jax.experimental import pallas as pl
from jax.experimental.pallas import tpu as pltpu
from jax.sharding import PartitionSpec as P

ADAPTER_SCALE = 0.25
MESH = pl.DeviceIdType.MESH
F32, BF16 = jnp.float32, jnp.bfloat16
FEATURES, TAIL, SLOTS, RANK = 3072, 128, 32, 64
SENDS, RECVS = 110, 130


def dot(a, b, over, precision=None):
    return lax.dot_general(
        a, b, ((over[:1], over[1:]), ((), ())), precision=precision, preferred_element_type=F32
    )


def layer_kernel(
    og_in,
    scores,
    idx,
    router,
    codes_in,
    scales,
    stored_in,
    ctx_in,
    down_in,
    up_in,
    hidden_out,
    token_out,
    up_out,
    down_out,
    og,
    codes,
    stored,
    ctx,
    down,
    up,
    rows,
    weight,
    prod_out,
    prod_in,
    hidden,
    token,
    pg_out,
    pg_in,
    adapt,
    a_twin,
    a_y_out,
    a_y_in,
    a_x_out,
    a_x_in,
    a_z_out,
    a_z_in,
    b_pad,
    b_twin,
    b_z_out,
    b_z_in,
    y_gather,
    x_gather,
    router_pad,
    send,
    recv,
    local,
):
    d, e, s = lax.axis_index("dp"), lax.axis_index("expert"), lax.axis_index("shard")
    y, c = e // 2, e % 2
    twin = (d, y * 2 + 1 - c, s)
    keeps = s // 8 == c

    barrier = pltpu.get_barrier_semaphore()
    for target in (
        twin,
        ((d + 1) % 4, e, s),
        ((d + 3) % 4, e, s),
        (d, (e + 2) % 8, s),
        (d, (e + 6) % 8, s),
        (d, e, (s + 1) % 16),
        (d, e, (s + 15) % 16),
    ):
        pl.semaphore_signal(barrier, inc=1, device_id=target, device_id_type=MESH)

    loads = []
    for i, (src, dst) in enumerate(
        (
            (codes_in.at[:, pl.ds(pl.multiple_of(d * 256, 256), 256)], codes),
            (og_in, og),
            (ctx_in, ctx),
            (down_in, down),
            (up_in, up),
            (stored_in, stored),
        )
    ):
        loads.append(pltpu.make_async_copy(src, dst, local.at[2 + i]))
        loads[-1].start()

    made = []
    used = [0, 0]

    def describe(src, dst, i, j, target):
        return pltpu.make_async_remote_copy(
            src_ref=src,
            dst_ref=dst,
            send_sem=send.at[i],
            recv_sem=recv.at[j],
            device_id=target,
            device_id_type=MESH,
        )

    def start(src, dst, target):
        one = describe(src, dst, used[0], used[1], target)
        used[0] += 1
        used[1] += 1
        one.start()
        made.append(one)
        return one

    def row_range(first, count, step):
        return pl.ds(pl.multiple_of(first, step), count)

    labels = lax.broadcasted_iota(jnp.int32, (8, 128), 0)
    first_choice, second_choice = idx[0:1, :], idx[1:2, :]
    choose_first, choose_second = labels == first_choice, labels == second_choice
    score = scores[...]
    chosen_first = jnp.sum(jnp.where(choose_first, score, 0.0), axis=0, keepdims=True)
    chosen_second = jnp.sum(jnp.where(choose_second, score, 0.0), axis=0, keepdims=True)
    first_prob = 1.0 / (1.0 + jnp.exp(chosen_second - chosen_first))
    second_prob = 1.0 - first_prob
    in_first = (first_choice == 0).astype(F32)
    in_second = (second_choice == 0).astype(F32)
    flag = in_first + in_second
    before = lax.broadcasted_iota(jnp.int32, (128, 128), 0) < lax.broadcasted_iota(
        jnp.int32, (128, 128), 1
    )
    slot = dot(
        jnp.broadcast_to(flag, (16, 128)).astype(BF16),
        jnp.where(before, 1.0, 0.0).astype(BF16),
        (1, 0),
    )[0:1, :]
    slot_labels = lax.broadcasted_iota(jnp.int32, (SLOTS, 128), 0).astype(F32)
    placement = jnp.where(slot == slot_labels, flag, 0.0)
    window_prob = jnp.where(in_first > 0.0, first_prob, second_prob).astype(BF16).astype(F32)

    quarter = pl.ds(pl.multiple_of(d * 256, 256), 256)
    factors = scales[:, quarter].astype(F32)
    loads[0].wait()
    for k in range(3):
        block = codes[64 * k : 64 * k + 64, :].astype(F32) * factors[k : k + 1, :]
        weight[row_range(s * 192 + 64 * k, 64, 64), :] = block.astype(BF16)

    f = d * (1 - c) + y * c
    g = y * (1 - c) + d * c

    def at_fg(ff, gg):
        return (ff * (1 - c) + gg * c, gg * (1 - c) + ff * c)

    def device_fg(ff, gg):
        dd, yy = at_fg(ff % 4, gg % 4)
        return (dd, yy * 2 + c, s)

    def slot_fg(ff, gg):
        dd, yy = at_fg(ff % 4, gg % 4)
        return (dd * 8 + yy * 2 + c) * SLOTS

    f_plus, f_minus = device_fg(f + 1, g), device_fg(f + 3, g)
    g_plus, g_minus = device_fg(f, g + 1), device_fg(f, g + 3)
    z_plus, z_minus = (d, e, (s + 1) % 16), (d, e, (s + 15) % 16)

    def pass_rows(ff, gg, target, part=None):
        first, count = slot_fg(ff, gg), SLOTS
        if part is not None:
            first, count = first + 16 * part, 16
        piece = rows.at[row_range(first, count, 16)]
        return start(piece, piece, target)

    def pass_weight(owner, part, target):
        piece = weight.at[row_range((owner % 16) * 192 + 96 * part, 96, 16)]
        return start(piece, piece, target)

    pl.semaphore_wait(barrier, 7)
    z_up = [[None, None] for _ in range(8)]
    z_down = [[None, None] for _ in range(8)]
    for part in range(2):
        z_up[0][part] = pass_weight(s, part, z_plus)
        z_down[0][part] = pass_weight(s, part, z_minus)
    own = row_range(slot_fg(f, g), SLOTS, SLOTS)
    loads[1].wait()
    rows[own, 0:FEATURES] = dot(placement.astype(BF16), og[...], (1, 0)).astype(BF16)
    rows[own, FEATURES : FEATURES + TAIL] = jnp.broadcast_to(
        jnp.sum(placement * window_prob, axis=1, keepdims=True), (SLOTS, TAIL)
    ).astype(BF16)
    to_f_plus = pass_rows(f, g, f_plus)
    to_f_minus = pass_rows(f, g, f_minus)
    g_up, g_down, g_up_half, g_down_half = [], [], [], []
    to_twin = []

    def spread_g(ff):
        g_up.append(pass_rows(ff, g, g_plus))
        g_down.append(pass_rows(ff, g, g_minus))
        to_twin.append(pass_rows(ff, g, twin))

    spread_g(f)

    for one in loads[2:]:
        one.wait()
    low_in = dot(ctx[...], down[...], (1, 1)).astype(BF16)
    low_grad = (ADAPTER_SCALE * dot(og[...], up[...], (1, 1))).astype(BF16)
    adapt[0:RANK, :] = dot(low_in, og[...], (0, 0))
    adapt[RANK : 2 * RANK, :] = dot(low_grad, ctx[...], (0, 0))
    half = FEATURES // 2
    to_twin_a = start(
        adapt.at[:, pl.ds(pl.multiple_of((1 - c) * half, half), half)], a_twin, twin
    )

    def ring_step(h):
        for part in range(2):
            for chain, turn, target in ((z_up, -1, z_plus), (z_down, 1, z_minus)):
                if chain[h][part] is None:
                    continue
                chain[h][part].wait_recv()
                further = h + 1 < 7 or (h + 1 == 7 and part == (0 if chain is z_up else 1))
                if further:
                    chain[h + 1][part] = pass_weight(s + 16 + turn * (h + 1), part, target)

    from_f = (f, f + 3, f + 1, f + 2)

    def take_g(i):
        g_up[i].wait_recv()
        g_up_half.append(pass_rows(from_f[i], g + 3, g_plus, 0))
        g_down[i].wait_recv()
        g_down_half.append(pass_rows(from_f[i], g + 1, g_minus, 1))
        to_twin.append(pass_rows(from_f[i], g + 3, twin))
        to_twin.append(pass_rows(from_f[i], g + 1, twin))

    def take_g_half(i):
        g_up_half[i].wait_recv()
        g_down_half[i].wait_recv()
        to_twin.append(pass_rows(from_f[i], g + 2, twin))

    ring_step(0)
    to_f_plus.wait_recv()
    f_up_half = pass_rows(f + 3, g, f_plus, 0)
    spread_g(f + 3)
    to_f_minus.wait_recv()
    f_down_half = pass_rows(f + 1, g, f_minus, 1)
    spread_g(f + 1)
    ring_step(1)
    take_g(0)
    f_up_half.wait_recv()
    f_down_half.wait_recv()
    spread_g(f + 2)
    ring_step(2)
    take_g_half(0)
    ring_step(3)
    take_g(1)
    ring_step(4)
    take_g(2)
    take_g_half(1)
    ring_step(5)

    to_twin_a.wait_recv()
    a_twin[...] += adapt[:, pl.ds(pl.multiple_of(c * half, half), half)]
    a_y_out[...] = a_twin[...].astype(BF16)

    take_g(3)
    take_g_half(2)
    ring_step(6)
    take_g_half(3)
    a_y = []
    for j in range(1, 4):
        to = (y + j) % 4
        a_y.append(
            start(a_y_out.at[row_range(to * 32, 32, 32)], a_y_in.at[j - 1], (d, to * 2 + c, s))
        )
    for k in range(16):
        router_pad[k] = router[:, 192 * k : 192 * k + 192].astype(F32)
    up_router = dot(up[...], router[...], (1, 1))
    ring_step(7)
    for one in to_twin:
        one.wait_recv()

    exchange = []
    for j in (2, 1, 3, 0):
        to = (d + j) % 4
        product = dot(
            rows[row_range(to * 256, 256, 256), 0:FEATURES], weight[...], (1, 0)
        ).astype(BF16)
        if j == 0:
            prod_in[d] = product
        else:
            prod_out[to] = product
            exchange.append((j, start(prod_out.at[to], prod_in.at[d], (to, e, s))))

    for one in a_y:
        one.wait_recv()
    a_x_out[...] = a_twin[row_range(y * 32, 32, 32), :]
    for j in range(3):
        a_x_out[...] += a_y_in[j].astype(F32)
    a_x = []
    for j in range(1, 4):
        to = (d + j) % 4
        a_x.append(start(a_x_out.at[row_range(to * 8, 8, 8)], a_x_in.at[j - 1], (to, e, s)))

    own_probs = rows[row_range(d * 256, 256, 256), FEATURES : FEATURES + TAIL].astype(F32)

    def take_product(q, first):
        total = None
        for k in range(2):
            columns = pl.ds(pl.multiple_of(q * 256 + 128 * k, 128), 128)
            piece = prod_in[q, :, 128 * k : 128 * k + 128].astype(F32)
            hidden[:, columns] = (own_probs * piece).astype(BF16)
            term = stored[:, columns].astype(F32) * piece
            total = term if total is None else total + term
        if first:
            pg_out[...] = total
        else:
            pg_out[...] += total

    take_product(d, True)
    for j, one in exchange[1:] + exchange[:1]:
        one.wait_recv()
        take_product((d + 4 - j) % 4, False)
    hidden_copy = pltpu.make_async_copy(hidden, hidden_out, local.at[0])
    hidden_copy.start()

    pg = []
    for p in (4, 5, 3, 2, 6, 7, 1):
        to = (e + p) % 8
        pg.append(start(pg_out.at[row_range(to * 32, 32, 32)], pg_in.at[e], (d, to, s)))
    pg_in[e] = pg_out[row_range(e * 32, 32, 32), :]

    for one in a_x:
        one.wait_recv()
    part = a_x_out[row_range(d * 8, 8, 8), :] + a_x_in[0] + a_x_in[1] + a_x_in[2]
    for j in range(8):
        a_z_out[j, :, 0:192] = part[:, 192 * j : 192 * j + 192]
    a_z_out[:, :, 192:256] = jnp.zeros((8, 8, 64), F32)

    def over_z(out, landing):
        first_send, first_recv = used
        used[0] += 8
        used[1] += 16
        for j in range(8):
            k = c * 8 + j

            @pl.when(k != s)
            def _():
                describe(
                    out.at[j], landing.at[s], first_send + j, first_recv + s, (d, e, k)
                ).start()

        return first_send, first_recv

    def sum_over_z(out, landing, first):
        landing[s] = out[s % 8]
        for i in range(16):

            @pl.when(i != s)
            def _():
                describe(out.at[0], landing.at[i], first[0], first[1] + i, z_plus).wait_recv()

        total = landing[0]
        for i in range(1, 16):
            total = total + landing[i]
        return total

    def sent_over_z(out, first):
        for j in range(8):

            @pl.when(c * 8 + j != s)
            def _():
                describe(out.at[j], out.at[j], first[0] + j, first[1], z_plus).wait_send()

    first_a = over_z(a_z_out, a_z_in)

    for one in pg:
        one.wait_recv()
    returned = pg_in[0]
    for k in range(1, 8):
        returned = returned + pg_in[k]
    returned = jnp.sum(returned, axis=1, keepdims=True)
    window_grad = jnp.sum(placement * returned, axis=0, keepdims=True)
    spread = first_prob * second_prob * (window_grad * in_first - window_grad * in_second)
    sign = choose_first.astype(F32) - choose_second.astype(F32)
    logit_grad = (spread * sign).astype(BF16)

    by_feature = dot(logit_grad, ctx[...], (1, 0))
    by_rank = dot(logit_grad, low_in, (1, 0))
    for k in range(16):
        b_pad[k, :, 0:192] = by_feature[:, 192 * k : 192 * k + 192]
        b_pad[k, :, 192:256] = by_rank
    to_twin_b = start(b_pad.at[row_range((1 - c) * 8, 8, 8)], b_twin, twin)
    token[...] = dot(logit_grad, router[...], (0, 0)).astype(BF16)
    token_copy = pltpu.make_async_copy(token, token_out, local.at[1])
    token_copy.start()
    to_twin_b.wait_recv()
    b_z_out[...] = b_pad[row_range(c * 8, 8, 8)] + b_twin[...]
    first_b = over_z(b_z_out, b_z_in)

    first_y = list(used)
    first_x = [used[0] + 3, used[1] + 3]
    last = [used[0] + 6, used[1] + 6]

    @pl.when(keeps)
    def _():
        y_gather[y, 0:8, :] = sum_over_z(a_z_out, a_z_in, first_a)
        y_gather[y, 8:16, :] = sum_over_z(b_z_out, b_z_in, first_b)
        copies = []
        for j in range(1, 4):
            copies.append(
                describe(
                    y_gather.at[y],
                    y_gather.at[y],
                    first_y[0] + j - 1,
                    first_y[1] + j - 1,
                    (d, ((y + j) % 4) * 2 + c, s),
                )
            )
        for one in copies:
            one.start()
        for one in copies:
            one.wait_recv()
        for k in range(4):
            x_gather[d, 8 * k : 8 * k + 8, :] = y_gather[k, 0:8, :]
        x_gather[d, 32:40, :] = (
            y_gather[0, 8:16, :] + y_gather[1, 8:16, :] + y_gather[2, 8:16, :] + y_gather[3, 8:16, :]
        )
        for j in range(1, 4):
            copies.append(
                describe(
                    x_gather.at[d],
                    x_gather.at[d],
                    first_x[0] + j - 1,
                    first_x[1] + j - 1,
                    ((d + j) % 4, e, s),
                )
            )
        for one in copies[3:]:
            one.start()
        for one in copies[3:]:
            one.wait_recv()
        across = describe(x_gather, x_gather, last[0], last[1], twin)
        across.start()
        across.wait_send()
        for one in copies:
            one.wait_send()

    @pl.when(jnp.logical_not(keeps))
    def _():
        describe(x_gather, x_gather, last[0], last[1], twin).wait_recv()

    total = (
        x_gather[0, 32:40, :] + x_gather[1, 32:40, :] + x_gather[2, 32:40, :] + x_gather[3, 32:40, :]
    )
    exact = lax.Precision.HIGHEST
    more_up = dot(total[:, 192:256], router_pad[s], (0, 0), exact)
    more_down = dot(up_router, total[:, 0:192], (1, 0), exact)
    for k in range(4):
        for j in range(4):
            first = 32 * k + 8 * j
            block = x_gather[j, 8 * k : 8 * k + 8, 0:192]
            if k < 2:
                up_out[first : first + 8, :] = ADAPTER_SCALE * (block + more_up[first : first + 8])
            else:
                first = first - RANK
                down_out[first : first + 8, :] = block + ADAPTER_SCALE * more_down[first : first + 8]

    sent_over_z(a_z_out, first_a)
    sent_over_z(b_z_out, first_b)
    for one in made:
        one.wait_send()
    hidden_copy.wait()
    token_copy.wait()


def finish_kernel(*refs):
    sources, targets, held, done = refs[:4], refs[4:8], refs[8:12], refs[12]
    loads = [pltpu.make_async_copy(sources[i], held[i], done.at[0, i]) for i in range(4)]
    stores = [pltpu.make_async_copy(held[i], targets[i], done.at[1, i]) for i in range(4)]
    for one in loads:
        one.start()
    for load, store in zip(loads, stores):
        load.wait()
        store.start()
    for one in stores:
        one.wait()


def per_device(og, scores, idx, router, codes, scales, stored, ctx, down, up):
    vmem = pl.BlockSpec(memory_space=pltpu.VMEM)
    anywhere = pl.BlockSpec(memory_space=pl.ANY)
    shape = jax.ShapeDtypeStruct
    results = (
        shape((256, 1024), BF16),
        shape((128, FEATURES), BF16),
        shape((RANK, 192), F32),
        shape((RANK, 192), F32),
    )
    made = pl.pallas_call(
        layer_kernel,
        out_shape=results,
        in_specs=[anywhere, vmem, vmem, vmem, anywhere, vmem] + [anywhere] * 4,
        out_specs=(anywhere, anywhere, vmem, vmem),
        scratch_shapes=[
            pltpu.VMEM((128, FEATURES), BF16),
            pltpu.VMEM((192, 256), BF16),
            pltpu.VMEM((256, 1024), BF16),
            pltpu.VMEM((128, FEATURES), BF16),
            pltpu.VMEM((RANK, FEATURES), BF16),
            pltpu.VMEM((RANK, FEATURES), BF16),
            pltpu.VMEM((1024, FEATURES + TAIL), BF16),
            pltpu.VMEM((FEATURES, 256), BF16),
            pltpu.VMEM((4, 256, 256), BF16),
            pltpu.VMEM((4, 256, 256), BF16),
            pltpu.VMEM((256, 1024), BF16),
            pltpu.VMEM((128, FEATURES), BF16),
            pltpu.VMEM((256, 128), F32),
            pltpu.VMEM((8, 32, 128), F32),
            pltpu.VMEM((128, FEATURES), F32),
            pltpu.VMEM((128, FEATURES // 2), F32),
            pltpu.VMEM((128, FEATURES // 2), BF16),
            pltpu.VMEM((3, 32, FEATURES // 2), BF16),
            pltpu.VMEM((32, FEATURES // 2), F32),
            pltpu.VMEM((3, 8, FEATURES // 2), F32),
            pltpu.VMEM((8, 8, 256), F32),
            pltpu.VMEM((16, 8, 256), F32),
            pltpu.VMEM((16, 8, 256), F32),
            pltpu.VMEM((8, 8, 256), F32),
            pltpu.VMEM((8, 8, 256), F32),
            pltpu.VMEM((16, 8, 256), F32),
            pltpu.VMEM((4, 16, 256), F32),
            pltpu.VMEM((4, 40, 256), F32),
            pltpu.VMEM((16, 8, 192), F32),
            pltpu.SemaphoreType.DMA((SENDS,)),
            pltpu.SemaphoreType.DMA((RECVS,)),
            pltpu.SemaphoreType.DMA((8,)),
        ],
        compiler_params=pltpu.CompilerParams(
            collective_id=0, has_side_effects=True, vmem_limit_bytes=62 << 20
        ),
    )(og, scores.T, idx.T, router, codes, scales, stored[0, 0], ctx, down, up)
    hidden_grad, token_grad, up_gradient, grad_down = pl.pallas_call(
        finish_kernel,
        out_shape=results,
        in_specs=[anywhere] * 4,
        out_specs=(anywhere,) * 4,
        scratch_shapes=[pltpu.VMEM(one.shape, one.dtype) for one in results]
        + [pltpu.SemaphoreType.DMA((2, 4))],
        compiler_params=pltpu.CompilerParams(vmem_limit_bytes=62 << 20),
    )(*made)
    return hidden_grad.reshape(stored.shape), token_grad, grad_down, up_gradient


def solution(mesh):
    tokens = P(("dp", "expert", "shard"), None)
    blocks = P("shard", "expert")
    hidden = P("dp", "shard", None, "expert")
    shares = P(None, "shard")
    return jax.shard_map(
        per_device,
        mesh=mesh,
        in_specs=(tokens, tokens, tokens, P(), blocks, blocks, hidden, tokens, P(), P()),
        out_specs=(hidden, tokens, shares, shares),
        check_vma=False,
    )
```

```python
import jax
import jax.numpy as jnp
from jax import lax
from jax.experimental import pallas as pl
from jax.experimental.pallas import tpu as pltpu
from jax.sharding import PartitionSpec as P

ADAPTER_SCALE = 0.25
MESH = pl.DeviceIdType.MESH
F32, BF16 = jnp.float32, jnp.bfloat16
FEATURES, TAIL, SLOTS, RANK = 3072, 128, 32, 64
SENDS, RECVS = 120, 140


def dot(a, b, over, precision=None):
    return lax.dot_general(
        a, b, ((over[:1], over[1:]), ((), ())), precision=precision, preferred_element_type=F32
    )


def layer_kernel(
    og_in,
    scores,
    idx,
    router,
    codes_in,
    scales,
    stored_in,
    ctx_in,
    down_in,
    up_in,
    hidden_out,
    token_out,
    up_out,
    down_out,
    og,
    codes,
    stored,
    ctx,
    down,
    up,
    rows,
    weight,
    prod_out,
    prod_in,
    hidden,
    token,
    pg_out,
    pg_in,
    adapt,
    a_twin,
    a_y_out,
    a_y_in,
    a_x_out,
    a_x_in,
    a_z_out,
    a_z_in,
    b_pad,
    b_twin,
    b_z_out,
    b_z_in,
    a_y_gather,
    a_x_gather,
    b_y_gather,
    b_x_gather,
    router_pad,
    twin_probs,
    send,
    recv,
    local,
):
    d, e, s = lax.axis_index("dp"), lax.axis_index("expert"), lax.axis_index("shard")
    y, c = e // 2, e % 2
    twin = (d, y * 2 + 1 - c, s)
    keeps = s // 8 == c

    barrier = pltpu.get_barrier_semaphore()
    for target in (
        twin,
        ((d + 1) % 4, e, s),
        ((d + 3) % 4, e, s),
        (d, (e + 2) % 8, s),
        (d, (e + 6) % 8, s),
        (d, y * 2, (s + 1) % 16),
        (d, y * 2 + 1, (s + 1) % 16),
        (d, y * 2, (s + 15) % 16),
        (d, y * 2 + 1, (s + 15) % 16),
    ):
        pl.semaphore_signal(barrier, inc=1, device_id=target, device_id_type=MESH)

    loads = []
    for i, (src, dst) in enumerate(
        (
            (codes_in.at[:, pl.ds(pl.multiple_of(d * 256, 256), 256)], codes),
            (og_in, og),
            (ctx_in, ctx),
            (down_in, down),
            (up_in, up),
            (stored_in, stored),
        )
    ):
        loads.append(pltpu.make_async_copy(src, dst, local.at[2 + i]))
        loads[-1].start()

    made = []
    used = [0, 0]

    def describe(src, dst, i, j, target):
        return pltpu.make_async_remote_copy(
            src_ref=src,
            dst_ref=dst,
            send_sem=send.at[i],
            recv_sem=recv.at[j],
            device_id=target,
            device_id_type=MESH,
        )

    def start(src, dst, target):
        one = describe(src, dst, used[0], used[1], target)
        used[0] += 1
        used[1] += 1
        one.start()
        made.append(one)
        return one

    def row_range(first, count, step):
        return pl.ds(pl.multiple_of(first, step), count)

    labels = lax.broadcasted_iota(jnp.int32, (8, 128), 0)
    first_choice, second_choice = idx[0:1, :], idx[1:2, :]
    choose_first, choose_second = labels == first_choice, labels == second_choice
    score = scores[...]
    chosen_first = jnp.sum(jnp.where(choose_first, score, 0.0), axis=0, keepdims=True)
    chosen_second = jnp.sum(jnp.where(choose_second, score, 0.0), axis=0, keepdims=True)
    first_prob = 1.0 / (1.0 + jnp.exp(chosen_second - chosen_first))
    second_prob = 1.0 - first_prob
    in_first = (first_choice == 0).astype(F32)
    in_second = (second_choice == 0).astype(F32)
    flag = in_first + in_second
    before = lax.broadcasted_iota(jnp.int32, (128, 128), 0) < lax.broadcasted_iota(
        jnp.int32, (128, 128), 1
    )
    slot = dot(
        jnp.broadcast_to(flag, (16, 128)).astype(BF16),
        jnp.where(before, 1.0, 0.0).astype(BF16),
        (1, 0),
    )[0:1, :]
    slot_labels = lax.broadcasted_iota(jnp.int32, (SLOTS, 128), 0).astype(F32)
    placement = jnp.where(slot == slot_labels, flag, 0.0)
    window_prob = jnp.where(in_first > 0.0, first_prob, second_prob).astype(BF16).astype(F32)

    quarter = pl.ds(pl.multiple_of(d * 256, 256), 256)
    factors = scales[:, quarter].astype(F32)
    loads[0].wait()
    for k in range(3):
        block = codes[64 * k : 64 * k + 64, :].astype(F32) * factors[k : k + 1, :]
        weight[c, row_range(s * 192 + 64 * k, 64, 64), :] = block.astype(BF16)

    f = d * (1 - c) + y * c
    g = y * (1 - c) + d * c

    def at_fg(ff, gg):
        return (ff * (1 - c) + gg * c, gg * (1 - c) + ff * c)

    def device_fg(ff, gg):
        dd, yy = at_fg(ff % 4, gg % 4)
        return (dd, yy * 2 + c, s)

    f_plus, f_minus = device_fg(f + 1, g), device_fg(f + 3, g)
    g_plus, g_minus = device_fg(f, g + 1), device_fg(f, g + 3)
    z_plus = (d, e, (s + 1) % 16)

    def pass_rows(ff, gg, target, part=None):
        dd, yy = at_fg(ff % 4, gg % 4)
        piece = rows.at[dd, yy]
        if part is not None:
            piece = rows.at[dd, yy, pl.ds(16 * part, 16)]
        return start(piece, piece, target)

    def weight_piece(core, owner, part):
        return weight.at[core, row_range((owner % 16) * 192 + 96 * part, 96, 16)]

    turn = 1 - 2 * c
    onward = (d, e, (s + 16 + turn) % 16)
    pl.semaphore_wait(barrier, 9)
    own_up, own_down = [], []
    for part in range(2):
        for core, step, made_first in ((0, 1, own_up), (1, 15, own_down)):
            made_first.append(tuple(used))
            used[0] += 1
            used[1] += 2
            piece = weight_piece(c, s, part)
            describe(
                piece,
                piece,
                made_first[-1][0],
                made_first[-1][1] + c,
                (d, y * 2 + core, (s + step) % 16),
            ).start()
    piece = weight.at[c, row_range(s * 192, 192, 64)]
    weights_to_twin = [start(piece, piece, twin)]
    passing = {}

    def ring_step(h):
        owner = s + 16 - turn * h
        arrived = dict(passing)
        passing.clear()
        for part in range(2):
            for core in range(2):
                if h == 1:
                    first = own_up[part][1] * (1 - c) + own_down[part][1] * c + core
                    piece = weight_piece(core, owner, part)
                    describe(piece, piece, 0, first, twin).wait_recv()
                elif (core, part) in arrived:
                    arrived[core, part].wait_recv()
                if h < 7:
                    piece = weight_piece(core, owner, part)
                    passing[core, part] = start(piece, piece, onward)
                elif h == 7 and core == 1:
                    piece = weight_piece(c, owner, part)
                    passing[core, part] = start(piece, piece, onward)
        rows_of_owner = row_range((owner % 16) * 192, 192, 64)
        piece = weight.at[:, rows_of_owner] if h < 8 else weight.at[c, rows_of_owner]
        weights_to_twin.append(start(piece, piece, twin))

    loads[1].wait()
    rows[d, y, :, 0:FEATURES] = dot(placement.astype(BF16), og[...], (1, 0)).astype(BF16)
    rows[d, y, :, FEATURES : FEATURES + TAIL] = jnp.broadcast_to(
        jnp.sum(placement * window_prob, axis=1, keepdims=True), (SLOTS, TAIL)
    ).astype(BF16)
    to_f_plus = pass_rows(f, g, f_plus)
    to_f_minus = pass_rows(f, g, f_minus)
    g_up, g_down, g_up_half, g_down_half = [], [], [], []

    def spread_g(ff):
        g_up.append(pass_rows(ff, g, g_plus))
        g_down.append(pass_rows(ff, g, g_minus))

    spread_g(f)

    for one in loads[2:]:
        one.wait()
    low_in = dot(ctx[...], down[...], (1, 1)).astype(BF16)
    low_grad = (ADAPTER_SCALE * dot(og[...], up[...], (1, 1))).astype(BF16)
    adapt[0:RANK, :] = dot(low_in, og[...], (0, 0))
    adapt[RANK : 2 * RANK, :] = dot(low_grad, ctx[...], (0, 0))
    half = FEATURES // 2
    to_twin_a = start(
        adapt.at[:, pl.ds(pl.multiple_of((1 - c) * half, half), half)], a_twin, twin
    )

    from_f = (f, f + 3, f + 1, f + 2)

    def take_g(i):
        g_up[i].wait_recv()
        g_up_half.append(pass_rows(from_f[i], g + 3, g_plus, 0))
        g_down[i].wait_recv()
        g_down_half.append(pass_rows(from_f[i], g + 1, g_minus, 1))

    def take_g_half(i):
        g_up_half[i].wait_recv()
        g_down_half[i].wait_recv()

    ring_step(1)
    to_f_plus.wait_recv()
    f_up_half = pass_rows(f + 3, g, f_plus, 0)
    spread_g(f + 3)
    to_f_minus.wait_recv()
    f_down_half = pass_rows(f + 1, g, f_minus, 1)
    spread_g(f + 1)
    ring_step(2)
    take_g(0)
    ring_step(3)
    f_up_half.wait_recv()
    f_down_half.wait_recv()
    spread_g(f + 2)
    ring_step(4)
    take_g_half(0)
    probs_to_twin = start(rows.at[d, :, :, pl.ds(FEATURES, TAIL)], twin_probs, twin)

    to_twin_a.wait_recv()
    a_twin[...] += adapt[:, pl.ds(pl.multiple_of(c * half, half), half)]
    a_y_out[...] = a_twin[...].astype(BF16)
    a_y = []
    for j in range(1, 4):
        to = (y + j) % 4
        a_y.append(
            start(a_y_out.at[row_range(to * 32, 32, 32)], a_y_in.at[j - 1], (d, to * 2 + c, s))
        )

    ring_step(5)
    take_g(1)
    ring_step(6)
    take_g(2)
    ring_step(7)
    take_g_half(1)

    for one in a_y:
        one.wait_recv()
    a_x_out[...] = a_twin[row_range(y * 32, 32, 32), :]
    for j in range(3):
        a_x_out[...] += a_y_in[j].astype(F32)
    a_x = []
    for j in range(1, 4):
        to = (d + j) % 4
        a_x.append(start(a_x_out.at[row_range(to * 8, 8, 8)], a_x_in.at[j - 1], (to, e, s)))

    ring_step(8)
    take_g(3)
    take_g_half(2)
    take_g_half(3)
    for k in range(16):
        router_pad[k] = router[:, 192 * k : 192 * k + 192].astype(F32)
    up_router = dot(up[...], router[...], (1, 1))
    for one in weights_to_twin:
        one.wait_recv()

    left = rows[:, :, :, 0:FEATURES].reshape(16 * SLOTS, FEATURES)
    exchange = []
    for k in range(2):
        core = (c + 1 + k) % 2
        product = dot(left, weight[core], (1, 0)).astype(BF16)
        prod_out[k] = product.reshape(4, 128, 256)
        for j in (2, 1, 3, 0):
            to = (d + j) % 4
            if j == 0 and k == 1:
                prod_in[d, c] = prod_out[k, d]
            else:
                exchange.append(
                    (j, k, start(prod_out.at[k, to], prod_in.at[d, c], (to, y * 2 + core, s)))
                )

    for one in a_x:
        one.wait_recv()
    part = a_x_out[row_range(d * 8, 8, 8), :] + a_x_in[0] + a_x_in[1] + a_x_in[2]
    for j in range(8):
        a_z_out[j, :, 0:192] = part[:, 192 * j : 192 * j + 192]
    a_z_out[:, :, 192:256] = jnp.zeros((8, 8, 64), F32)

    def over_z(out, landing):
        first_send, first_recv = used
        used[0] += 8
        used[1] += 16
        for j in range(8):
            k = c * 8 + j

            @pl.when(k != s)
            def _():
                describe(
                    out.at[j], landing.at[s], first_send + j, first_recv + s, (d, e, k)
                ).start()

        return first_send, first_recv

    def sum_over_z(out, landing, first):
        landing[s] = out[s % 8]
        for i in range(16):

            @pl.when(i != s)
            def _():
                describe(out.at[0], landing.at[i], first[0], first[1] + i, z_plus).wait_recv()

        total = landing[0]
        for i in range(1, 16):
            total = total + landing[i]
        return total

    def sent_over_z(out, first):
        for j in range(8):

            @pl.when(c * 8 + j != s)
            def _():
                describe(out.at[j], out.at[j], first[0] + j, first[1], z_plus).wait_send()

    first_a = over_z(a_z_out, a_z_in)

    probs_to_twin.wait_recv()

    def take_product(q, same, first):
        core = c if same else 1 - c
        for k in range(4):
            place = pl.ds(pl.multiple_of(64 * k + 32 * core, 32), SLOTS)
            prob = rows[d, k, :, FEATURES : FEATURES + TAIL] if same else twin_probs[k]
            prob = prob.astype(F32)
            total = None
            for n in range(2):
                columns = pl.ds(pl.multiple_of(q * 256 + 128 * n, 128), 128)
                piece = prod_in[q, core, 32 * k : 32 * k + 32, 128 * n : 128 * n + 128].astype(F32)
                hidden[place, columns] = (prob * piece).astype(BF16)
                term = stored[place, columns].astype(F32) * piece
                total = term if total is None else total + term
            if first:
                pg_out[place, :] = total
            else:
                pg_out[place, :] += total

    take_product(d, True, True)
    order = {(1, 0): 0, (3, 0): 1, (0, 0): 2, (2, 0): 3, (1, 1): 4, (3, 1): 5, (2, 1): 6}
    for j, k, one in sorted(exchange, key=lambda item: order[item[:2]]):
        one.wait_recv()
        take_product((d + 4 - j) % 4, k == 1, (j, k) == (1, 0))
    hidden_copy = pltpu.make_async_copy(hidden, hidden_out, local.at[0])
    hidden_copy.start()

    pg = []
    for p in (4, 5, 3, 2, 6, 7, 1):
        to = (e + p) % 8
        pg.append(start(pg_out.at[row_range(to * 32, 32, 32)], pg_in.at[e], (d, to, s)))
    pg_in[e] = pg_out[row_range(e * 32, 32, 32), :]

    def reserve(sends, recvs):
        first = tuple(used)
        used[0] += sends
        used[1] += recvs
        return first

    def along(buffer, first, axis):
        mine, copies = (y if axis == "y" else d), []
        for j in range(1, 4):
            to = (d, ((y + j) % 4) * 2 + c, s) if axis == "y" else ((d + j) % 4, e, s)
            piece = buffer.at[mine]
            copies.append(describe(piece, piece, first[0] + j - 1, first[1] + j - 1, to))
        return copies

    sems_a_y, sems_a_x, sems_a_twin = reserve(3, 3), reserve(3, 3), reserve(1, 1)
    sems_b_y, sems_b_x = reserve(3, 3), reserve(7, 4)

    @pl.when(keeps)
    def _():
        a_y_gather[y] = sum_over_z(a_z_out, a_z_in, first_a)
        for one in along(a_y_gather, sems_a_y, "y"):
            one.start()

    for one in pg:
        one.wait_recv()
    returned = pg_in[0]
    for k in range(1, 8):
        returned = returned + pg_in[k]
    returned = jnp.sum(returned, axis=1, keepdims=True)
    window_grad = jnp.sum(placement * returned, axis=0, keepdims=True)
    spread = first_prob * second_prob * (window_grad * in_first - window_grad * in_second)
    sign = choose_first.astype(F32) - choose_second.astype(F32)
    logit_grad = (spread * sign).astype(BF16)

    by_feature = dot(logit_grad, ctx[...], (1, 0))
    by_rank = dot(logit_grad, low_in, (1, 0))
    for k in range(16):
        b_pad[k, :, 0:192] = by_feature[:, 192 * k : 192 * k + 192]
        b_pad[k, :, 192:256] = by_rank
    to_twin_b = start(b_pad.at[row_range((1 - c) * 8, 8, 8)], b_twin, twin)
    token[...] = dot(logit_grad, router[...], (0, 0)).astype(BF16)
    token_copy = pltpu.make_async_copy(token, token_out, local.at[1])
    token_copy.start()
    to_twin_b.wait_recv()
    b_z_out[...] = b_pad[row_range(c * 8, 8, 8)] + b_twin[...]
    first_b = over_z(b_z_out, b_z_in)

    a_across = describe(a_x_gather, a_x_gather, sems_a_twin[0], sems_a_twin[1], twin)

    @pl.when(keeps)
    def _():
        for one in along(a_y_gather, sems_a_y, "y"):
            one.wait()
        for k in range(4):
            a_x_gather[d, 8 * k : 8 * k + 8, :] = a_y_gather[k]
        copies = along(a_x_gather, sems_a_x, "x")
        for one in copies:
            one.start()

    for made_first in own_up + own_down:
        piece = weight_piece(c, s, 0)
        describe(piece, piece, made_first[0], 0, twin).wait_send()
    for one in made:
        one.wait_send()
    sent_over_z(a_z_out, first_a)
    hidden_copy.wait()

    @pl.when(keeps)
    def _():
        for one in along(a_x_gather, sems_a_x, "x"):
            one.wait()
        a_across.start()
        b_y_gather[y] = sum_over_z(b_z_out, b_z_in, first_b)
        by_y = along(b_y_gather, sems_b_y, "y")
        for one in by_y:
            one.start()
        for one in by_y:
            one.wait_recv()
        b_x_gather[d] = b_y_gather[0] + b_y_gather[1] + b_y_gather[2] + b_y_gather[3]
        piece = b_x_gather.at[d]
        by_x = []
        for j in (2, 1, 3, 0):
            for core in (c, 1 - c):
                if j == 0 and core is c:
                    continue
                target = ((d + j) % 4, y * 2 + core, s)
                by_x.append(
                    describe(piece, piece, sems_b_x[0] + len(by_x), sems_b_x[1] + d, target)
                )
        for one in by_x:
            one.start()
        for q in range(4):

            @pl.when(q != d)
            def _():
                slot = b_x_gather.at[q]
                describe(slot, slot, sems_b_x[0], sems_b_x[1] + q, twin).wait_recv()

        for one in by_x + by_y:
            one.wait_send()
        a_across.wait_send()

    @pl.when(jnp.logical_not(keeps))
    def _():
        a_across.wait_recv()
        for q in range(4):
            slot = b_x_gather.at[q]
            describe(slot, slot, sems_b_x[0], sems_b_x[1] + q, twin).wait_recv()

    total = b_x_gather[0] + b_x_gather[1] + b_x_gather[2] + b_x_gather[3]
    exact = lax.Precision.HIGHEST
    more_up = dot(total[:, 192:256], router_pad[s], (0, 0), exact)
    more_down = dot(up_router, total[:, 0:192], (1, 0), exact)
    for k in range(4):
        for j in range(4):
            first = 32 * k + 8 * j
            block = a_x_gather[j, 8 * k : 8 * k + 8, 0:192]
            if k < 2:
                up_out[first : first + 8, :] = ADAPTER_SCALE * (block + more_up[first : first + 8])
            else:
                first = first - RANK
                down_out[first : first + 8, :] = block + ADAPTER_SCALE * more_down[first : first + 8]

    sent_over_z(b_z_out, first_b)
    token_copy.wait()


def finish_kernel(*refs):
    sources, targets, held, done = refs[:4], refs[4:8], refs[8:12], refs[12]
    loads = [pltpu.make_async_copy(sources[i], held[i], done.at[0, i]) for i in range(4)]
    stores = [pltpu.make_async_copy(held[i], targets[i], done.at[1, i]) for i in range(4)]
    for one in loads:
        one.start()
    for load, store in zip(loads, stores):
        load.wait()
        store.start()
    for one in stores:
        one.wait()


def per_device(og, scores, idx, router, codes, scales, stored, ctx, down, up):
    vmem = pl.BlockSpec(memory_space=pltpu.VMEM)
    anywhere = pl.BlockSpec(memory_space=pl.ANY)
    shape = jax.ShapeDtypeStruct
    results = (
        shape((256, 1024), BF16),
        shape((128, FEATURES), BF16),
        shape((RANK, 192), F32),
        shape((RANK, 192), F32),
    )
    made = pl.pallas_call(
        layer_kernel,
        out_shape=results,
        in_specs=[anywhere, vmem, vmem, vmem, anywhere, vmem] + [anywhere] * 4,
        out_specs=(anywhere, anywhere, vmem, vmem),
        scratch_shapes=[
            pltpu.VMEM((128, FEATURES), BF16),
            pltpu.VMEM((192, 256), BF16),
            pltpu.VMEM((256, 1024), BF16),
            pltpu.VMEM((128, FEATURES), BF16),
            pltpu.VMEM((RANK, FEATURES), BF16),
            pltpu.VMEM((RANK, FEATURES), BF16),
            pltpu.VMEM((4, 4, SLOTS, FEATURES + TAIL), BF16),
            pltpu.VMEM((2, FEATURES, 256), BF16),
            pltpu.VMEM((2, 4, 128, 256), BF16),
            pltpu.VMEM((4, 2, 128, 256), BF16),
            pltpu.VMEM((256, 1024), BF16),
            pltpu.VMEM((128, FEATURES), BF16),
            pltpu.VMEM((256, 128), F32),
            pltpu.VMEM((8, 32, 128), F32),
            pltpu.VMEM((128, FEATURES), F32),
            pltpu.VMEM((128, FEATURES // 2), F32),
            pltpu.VMEM((128, FEATURES // 2), BF16),
            pltpu.VMEM((3, 32, FEATURES // 2), BF16),
            pltpu.VMEM((32, FEATURES // 2), F32),
            pltpu.VMEM((3, 8, FEATURES // 2), F32),
            pltpu.VMEM((8, 8, 256), F32),
            pltpu.VMEM((16, 8, 256), F32),
            pltpu.VMEM((16, 8, 256), F32),
            pltpu.VMEM((8, 8, 256), F32),
            pltpu.VMEM((8, 8, 256), F32),
            pltpu.VMEM((16, 8, 256), F32),
            pltpu.VMEM((4, 8, 256), F32),
            pltpu.VMEM((4, 32, 256), F32),
            pltpu.VMEM((4, 8, 256), F32),
            pltpu.VMEM((4, 8, 256), F32),
            pltpu.VMEM((16, 8, 192), F32),
            pltpu.VMEM((4, SLOTS, TAIL), BF16),
            pltpu.SemaphoreType.DMA((SENDS,)),
            pltpu.SemaphoreType.DMA((RECVS,)),
            pltpu.SemaphoreType.DMA((8,)),
        ],
        compiler_params=pltpu.CompilerParams(
            collective_id=0, has_side_effects=True, vmem_limit_bytes=62 << 20
        ),
    )(og, scores.T, idx.T, router, codes, scales, stored[0, 0], ctx, down, up)
    hidden_grad, token_grad, up_gradient, grad_down = pl.pallas_call(
        finish_kernel,
        out_shape=results,
        in_specs=[anywhere] * 4,
        out_specs=(anywhere,) * 4,
        scratch_shapes=[pltpu.VMEM(one.shape, one.dtype) for one in results]
        + [pltpu.SemaphoreType.DMA((2, 4))],
        compiler_params=pltpu.CompilerParams(vmem_limit_bytes=62 << 20),
    )(*made)
    return hidden_grad.reshape(stored.shape), token_grad, grad_down, up_gradient


def solution(mesh):
    tokens = P(("dp", "expert", "shard"), None)
    blocks = P("shard", "expert")
    hidden = P("dp", "shard", None, "expert")
    shares = P(None, "shard")
    return jax.shard_map(
        per_device,
        mesh=mesh,
        in_specs=(tokens, tokens, tokens, P(), blocks, blocks, hidden, tokens, P(), P()),
        out_specs=(hidden, tokens, shares, shares),
        check_vma=False,
    )
```

```python
import jax
import jax.numpy as jnp
from jax import lax
from jax.experimental import pallas as pl
from jax.experimental.pallas import tpu as pltpu
from jax.sharding import PartitionSpec as P

ADAPTER_SCALE = 0.25
MESH = pl.DeviceIdType.MESH
F32, BF16 = jnp.float32, jnp.bfloat16
FEATURES, TAIL, SLOTS, RANK = 3072, 128, 32, 64
SENDS, RECVS = 120, 140


def dot(a, b, over, precision=None):
    return lax.dot_general(
        a, b, ((over[:1], over[1:]), ((), ())), precision=precision, preferred_element_type=F32
    )


def layer_kernel(
    og_in,
    scores_in,
    idx_in,
    router_in,
    codes_in,
    scales_in,
    stored_in,
    ctx_in,
    down_in,
    up_in,
    hidden_out,
    token_out,
    up_out,
    down_out,
    og,
    scores,
    idx,
    router,
    codes,
    scales,
    stored,
    ctx,
    down,
    up,
    rows,
    weight,
    prod_out,
    prod_in,
    hidden,
    token,
    pg_out,
    pg_in,
    adapt,
    a_twin,
    a_y_out,
    a_y_in,
    a_x_out,
    a_x_in,
    a_z_out,
    a_z_in,
    b_pad,
    b_twin,
    b_z_out,
    b_z_in,
    a_y_gather,
    a_x_gather,
    b_y_gather,
    b_x_gather,
    router_pad,
    twin_probs,
    send,
    recv,
    local,
):
    d, e, s = lax.axis_index("dp"), lax.axis_index("expert"), lax.axis_index("shard")
    y, c = e // 2, e % 2
    twin = (d, y * 2 + 1 - c, s)
    keeps = s // 8 == c

    barrier = pltpu.get_barrier_semaphore()
    for target in (
        twin,
        ((d + 1) % 4, e, s),
        ((d + 3) % 4, e, s),
        (d, (e + 2) % 8, s),
        (d, (e + 6) % 8, s),
        (d, y * 2, (s + 1) % 16),
        (d, y * 2 + 1, (s + 1) % 16),
        (d, y * 2, (s + 15) % 16),
        (d, y * 2 + 1, (s + 15) % 16),
    ):
        pl.semaphore_signal(barrier, inc=1, device_id=target, device_id_type=MESH)

    loads = []
    for i, (src, dst) in enumerate(
        (
            (codes_in.at[:, pl.ds(pl.multiple_of(d * 256, 256), 256)], codes),
            (scales_in, scales),
            (idx_in, idx),
            (scores_in, scores),
            (og_in, og),
            (ctx_in, ctx),
            (down_in, down),
            (up_in, up),
            (stored_in, stored),
            (router_in, router),
        )
    ):
        loads.append(pltpu.make_async_copy(src, dst, local.at[2 + i]))
        loads[-1].start()

    made = []
    used = [0, 0]

    def describe(src, dst, i, j, target):
        return pltpu.make_async_remote_copy(
            src_ref=src,
            dst_ref=dst,
            send_sem=send.at[i],
            recv_sem=recv.at[j],
            device_id=target,
            device_id_type=MESH,
        )

    def start(src, dst, target):
        one = describe(src, dst, used[0], used[1], target)
        used[0] += 1
        used[1] += 1
        one.start()
        made.append(one)
        return one

    def row_range(first, count, step):
        return pl.ds(pl.multiple_of(first, step), count)

    quarter = pl.ds(pl.multiple_of(d * 256, 256), 256)
    loads[0].wait()
    loads[1].wait()
    factors = scales[:, quarter].astype(F32)
    for k in range(3):
        block = codes[64 * k : 64 * k + 64, :].astype(F32) * factors[k : k + 1, :]
        weight[c, row_range(s * 192 + 64 * k, 64, 64), :] = block.astype(BF16)

    f = d * (1 - c) + y * c
    g = y * (1 - c) + d * c

    def at_fg(ff, gg):
        return (ff * (1 - c) + gg * c, gg * (1 - c) + ff * c)

    def device_fg(ff, gg):
        dd, yy = at_fg(ff % 4, gg % 4)
        return (dd, yy * 2 + c, s)

    f_plus, f_minus = device_fg(f + 1, g), device_fg(f + 3, g)
    g_plus, g_minus = device_fg(f, g + 1), device_fg(f, g + 3)
    z_plus = (d, e, (s + 1) % 16)

    def pass_rows(ff, gg, target, part=None):
        dd, yy = at_fg(ff % 4, gg % 4)
        piece = rows.at[dd, yy]
        if part is not None:
            piece = rows.at[dd, yy, pl.ds(16 * part, 16)]
        return start(piece, piece, target)

    def weight_piece(core, owner, part):
        return weight.at[core, row_range((owner % 16) * 192 + 96 * part, 96, 16)]

    turn = 1 - 2 * c
    onward = (d, e, (s + 16 + turn) % 16)
    pl.semaphore_wait(barrier, 9)
    own_up, own_down = [], []
    for part in range(2):
        for core, step, made_first in ((0, 1, own_up), (1, 15, own_down)):
            made_first.append(tuple(used))
            used[0] += 1
            used[1] += 2
            piece = weight_piece(c, s, part)
            describe(
                piece,
                piece,
                made_first[-1][0],
                made_first[-1][1] + c,
                (d, y * 2 + core, (s + step) % 16),
            ).start()
    piece = weight.at[c, row_range(s * 192, 192, 64)]
    weights_to_twin = [start(piece, piece, twin)]
    passing = {}

    def ring_step(h):
        owner = s + 16 - turn * h
        arrived = dict(passing)
        passing.clear()
        for part in range(2):
            for core in range(2):
                if h == 1:
                    first = own_up[part][1] * (1 - c) + own_down[part][1] * c + core
                    piece = weight_piece(core, owner, part)
                    describe(piece, piece, 0, first, twin).wait_recv()
                elif (core, part) in arrived:
                    arrived[core, part].wait_recv()
                if h < 7:
                    piece = weight_piece(core, owner, part)
                    passing[core, part] = start(piece, piece, onward)
                elif h == 7 and core == 1:
                    piece = weight_piece(c, owner, part)
                    passing[core, part] = start(piece, piece, onward)
        rows_of_owner = row_range((owner % 16) * 192, 192, 64)
        piece = weight.at[:, rows_of_owner] if h < 8 else weight.at[c, rows_of_owner]
        weights_to_twin.append(start(piece, piece, twin))

    loads[2].wait()
    loads[3].wait()
    labels = lax.broadcasted_iota(jnp.int32, (8, 128), 0)
    first_choice, second_choice = idx[0:1, :], idx[1:2, :]
    choose_first, choose_second = labels == first_choice, labels == second_choice
    score = scores[...]
    chosen_first = jnp.sum(jnp.where(choose_first, score, 0.0), axis=0, keepdims=True)
    chosen_second = jnp.sum(jnp.where(choose_second, score, 0.0), axis=0, keepdims=True)
    first_prob = 1.0 / (1.0 + jnp.exp(chosen_second - chosen_first))
    second_prob = 1.0 - first_prob
    in_first = (first_choice == 0).astype(F32)
    in_second = (second_choice == 0).astype(F32)
    flag = in_first + in_second
    before = lax.broadcasted_iota(jnp.int32, (128, 128), 0) < lax.broadcasted_iota(
        jnp.int32, (128, 128), 1
    )
    slot = dot(
        jnp.broadcast_to(flag, (16, 128)).astype(BF16),
        jnp.where(before, 1.0, 0.0).astype(BF16),
        (1, 0),
    )[0:1, :]
    slot_labels = lax.broadcasted_iota(jnp.int32, (SLOTS, 128), 0).astype(F32)
    placement = jnp.where(slot == slot_labels, flag, 0.0)
    window_prob = jnp.where(in_first > 0.0, first_prob, second_prob).astype(BF16).astype(F32)

    loads[4].wait()
    rows[d, y, :, 0:FEATURES] = dot(placement.astype(BF16), og[...], (1, 0)).astype(BF16)
    rows[d, y, :, FEATURES : FEATURES + TAIL] = jnp.broadcast_to(
        jnp.sum(placement * window_prob, axis=1, keepdims=True), (SLOTS, TAIL)
    ).astype(BF16)
    to_f_plus = pass_rows(f, g, f_plus)
    to_f_minus = pass_rows(f, g, f_minus)
    g_up, g_down, g_up_half, g_down_half = [], [], [], []

    def spread_g(ff):
        g_up.append(pass_rows(ff, g, g_plus))
        g_down.append(pass_rows(ff, g, g_minus))

    spread_g(f)

    for one in loads[5:]:
        one.wait()
    low_in = dot(ctx[...], down[...], (1, 1)).astype(BF16)
    low_grad = (ADAPTER_SCALE * dot(og[...], up[...], (1, 1))).astype(BF16)

    from_f = (f, f + 3, f + 1, f + 2)

    def take_g(i):
        g_up[i].wait_recv()
        g_up_half.append(pass_rows(from_f[i], g + 3, g_plus, 0))
        g_down[i].wait_recv()
        g_down_half.append(pass_rows(from_f[i], g + 1, g_minus, 1))

    def take_g_half(i):
        g_up_half[i].wait_recv()
        g_down_half[i].wait_recv()

    ring_step(1)
    adapt[0:RANK, :] = dot(low_in, og[...], (0, 0))
    to_f_plus.wait_recv()
    f_up_half = pass_rows(f + 3, g, f_plus, 0)
    spread_g(f + 3)
    to_f_minus.wait_recv()
    f_down_half = pass_rows(f + 1, g, f_minus, 1)
    spread_g(f + 1)
    ring_step(2)
    adapt[RANK : 2 * RANK, :] = dot(low_grad, ctx[...], (0, 0))
    half = FEATURES // 2
    to_twin_a = start(
        adapt.at[:, pl.ds(pl.multiple_of((1 - c) * half, half), half)], a_twin, twin
    )
    take_g(0)
    ring_step(3)
    f_up_half.wait_recv()
    f_down_half.wait_recv()
    spread_g(f + 2)
    ring_step(4)
    take_g_half(0)
    probs_to_twin = start(rows.at[d, :, :, pl.ds(FEATURES, TAIL)], twin_probs, twin)

    to_twin_a.wait_recv()
    a_twin[...] += adapt[:, pl.ds(pl.multiple_of(c * half, half), half)]
    a_y_out[...] = a_twin[...].astype(BF16)
    a_y = []
    for j in range(1, 4):
        to = (y + j) % 4
        a_y.append(
            start(a_y_out.at[row_range(to * 32, 32, 32)], a_y_in.at[j - 1], (d, to * 2 + c, s))
        )

    ring_step(5)
    take_g(1)
    ring_step(6)
    take_g(2)
    ring_step(7)
    take_g_half(1)

    for one in a_y:
        one.wait_recv()
    a_x_out[...] = a_twin[row_range(y * 32, 32, 32), :]
    for j in range(3):
        a_x_out[...] += a_y_in[j].astype(F32)
    a_x = []
    for j in range(1, 4):
        to = (d + j) % 4
        a_x.append(start(a_x_out.at[row_range(to * 8, 8, 8)], a_x_in.at[j - 1], (to, e, s)))

    ring_step(8)
    take_g(3)
    take_g_half(2)
    take_g_half(3)
    for k in range(16):
        router_pad[k] = router[:, 192 * k : 192 * k + 192].astype(F32)
    up_router = dot(up[...], router[...], (1, 1))
    for one in weights_to_twin:
        one.wait_recv()

    left = rows[:, :, :, 0:FEATURES].reshape(16 * SLOTS, FEATURES)
    exchange = []
    for k in range(2):
        core = (c + 1 + k) % 2
        product = dot(left, weight[core], (1, 0)).astype(BF16)
        prod_out[k] = product.reshape(4, 128, 256)
        for j in (2, 1, 3, 0):
            to = (d + j) % 4
            if j == 0 and k == 1:
                prod_in[d, c] = prod_out[k, d]
            else:
                exchange.append(
                    (j, k, start(prod_out.at[k, to], prod_in.at[d, c], (to, y * 2 + core, s)))
                )

    for one in a_x:
        one.wait_recv()
    part = a_x_out[row_range(d * 8, 8, 8), :] + a_x_in[0] + a_x_in[1] + a_x_in[2]
    for j in range(8):
        a_z_out[j, :, 0:192] = part[:, 192 * j : 192 * j + 192]
    a_z_out[:, :, 192:256] = jnp.zeros((8, 8, 64), F32)

    def over_z(out, landing):
        first_send, first_recv = used
        used[0] += 8
        used[1] += 16
        for j in range(8):
            k = c * 8 + j

            @pl.when(k != s)
            def _():
                describe(
                    out.at[j], landing.at[s], first_send + j, first_recv + s, (d, e, k)
                ).start()

        return first_send, first_recv

    def sum_over_z(out, landing, first):
        landing[s] = out[s % 8]
        for i in range(16):

            @pl.when(i != s)
            def _():
                describe(out.at[0], landing.at[i], first[0], first[1] + i, z_plus).wait_recv()

        total = landing[0]
        for i in range(1, 16):
            total = total + landing[i]
        return total

    def sent_over_z(out, first):
        for j in range(8):

            @pl.when(c * 8 + j != s)
            def _():
                describe(out.at[j], out.at[j], first[0] + j, first[1], z_plus).wait_send()

    first_a = over_z(a_z_out, a_z_in)

    probs_to_twin.wait_recv()

    def take_product(q, same, first):
        core = c if same else 1 - c
        for k in range(4):
            place = pl.ds(pl.multiple_of(64 * k + 32 * core, 32), SLOTS)
            prob = rows[d, k, :, FEATURES : FEATURES + TAIL] if same else twin_probs[k]
            prob = prob.astype(F32)
            total = None
            for n in range(2):
                columns = pl.ds(pl.multiple_of(q * 256 + 128 * n, 128), 128)
                piece = prod_in[q, core, 32 * k : 32 * k + 32, 128 * n : 128 * n + 128].astype(F32)
                hidden[place, columns] = (prob * piece).astype(BF16)
                term = stored[place, columns].astype(F32) * piece
                total = term if total is None else total + term
            if first:
                pg_out[place, :] = total
            else:
                pg_out[place, :] += total

    take_product(d, True, True)
    order = {(1, 0): 0, (3, 0): 1, (0, 0): 2, (2, 0): 3, (1, 1): 4, (3, 1): 5, (2, 1): 6}
    for j, k, one in sorted(exchange, key=lambda item: order[item[:2]]):
        one.wait_recv()
        take_product((d + 4 - j) % 4, k == 1, (j, k) == (1, 0))
    hidden_copy = pltpu.make_async_copy(hidden, hidden_out, local.at[0])
    hidden_copy.start()

    pg = []
    for p in (4, 5, 3, 2, 6, 7, 1):
        to = (e + p) % 8
        pg.append(start(pg_out.at[row_range(to * 32, 32, 32)], pg_in.at[e], (d, to, s)))
    pg_in[e] = pg_out[row_range(e * 32, 32, 32), :]

    def reserve(sends, recvs):
        first = tuple(used)
        used[0] += sends
        used[1] += recvs
        return first

    def along(buffer, first, axis):
        mine, copies = (y if axis == "y" else d), []
        for j in range(1, 4):
            to = (d, ((y + j) % 4) * 2 + c, s) if axis == "y" else ((d + j) % 4, e, s)
            piece = buffer.at[mine]
            copies.append(describe(piece, piece, first[0] + j - 1, first[1] + j - 1, to))
        return copies

    sems_a_y, sems_a_x, sems_a_twin = reserve(3, 3), reserve(3, 3), reserve(1, 1)
    sems_b_y, sems_b_x = reserve(3, 3), reserve(7, 4)

    @pl.when(keeps)
    def _():
        a_y_gather[y] = sum_over_z(a_z_out, a_z_in, first_a)
        for one in along(a_y_gather, sems_a_y, "y"):
            one.start()

    for one in pg:
        one.wait_recv()
    returned = pg_in[0]
    for k in range(1, 8):
        returned = returned + pg_in[k]
    returned = jnp.sum(returned, axis=1, keepdims=True)
    window_grad = jnp.sum(placement * returned, axis=0, keepdims=True)
    spread = first_prob * second_prob * (window_grad * in_first - window_grad * in_second)
    sign = choose_first.astype(F32) - choose_second.astype(F32)
    logit_grad = (spread * sign).astype(BF16)

    by_feature = dot(logit_grad, ctx[...], (1, 0))
    by_rank = dot(logit_grad, low_in, (1, 0))
    for k in range(16):
        b_pad[k, :, 0:192] = by_feature[:, 192 * k : 192 * k + 192]
        b_pad[k, :, 192:256] = by_rank
    to_twin_b = start(b_pad.at[row_range((1 - c) * 8, 8, 8)], b_twin, twin)
    token[...] = dot(logit_grad, router[...], (0, 0)).astype(BF16)
    token_copy = pltpu.make_async_copy(token, token_out, local.at[1])
    token_copy.start()
    to_twin_b.wait_recv()
    b_z_out[...] = b_pad[row_range(c * 8, 8, 8)] + b_twin[...]
    first_b = over_z(b_z_out, b_z_in)

    a_across = describe(a_x_gather, a_x_gather, sems_a_twin[0], sems_a_twin[1], twin)

    @pl.when(keeps)
    def _():
        for one in along(a_y_gather, sems_a_y, "y"):
            one.wait()
        for k in range(4):
            a_x_gather[d, 8 * k : 8 * k + 8, :] = a_y_gather[k]
        copies = along(a_x_gather, sems_a_x, "x")
        for one in copies:
            one.start()

    for made_first in own_up + own_down:
        piece = weight_piece(c, s, 0)
        describe(piece, piece, made_first[0], 0, twin).wait_send()
    for one in made:
        one.wait_send()
    sent_over_z(a_z_out, first_a)
    hidden_copy.wait()

    @pl.when(keeps)
    def _():
        for one in along(a_x_gather, sems_a_x, "x"):
            one.wait()
        a_across.start()
        b_y_gather[y] = sum_over_z(b_z_out, b_z_in, first_b)
        by_y = along(b_y_gather, sems_b_y, "y")
        for one in by_y:
            one.start()
        for one in by_y:
            one.wait_recv()
        b_x_gather[d] = b_y_gather[0] + b_y_gather[1] + b_y_gather[2] + b_y_gather[3]
        piece = b_x_gather.at[d]
        by_x = []
        for j in (2, 1, 3, 0):
            for core in (c, 1 - c):
                if j == 0 and core is c:
                    continue
                target = ((d + j) % 4, y * 2 + core, s)
                by_x.append(
                    describe(piece, piece, sems_b_x[0] + len(by_x), sems_b_x[1] + d, target)
                )
        for one in by_x:
            one.start()
        for q in range(4):

            @pl.when(q != d)
            def _():
                slot = b_x_gather.at[q]
                describe(slot, slot, sems_b_x[0], sems_b_x[1] + q, twin).wait_recv()

        for one in by_x + by_y:
            one.wait_send()
        a_across.wait_send()

    @pl.when(jnp.logical_not(keeps))
    def _():
        a_across.wait_recv()
        for q in range(4):
            slot = b_x_gather.at[q]
            describe(slot, slot, sems_b_x[0], sems_b_x[1] + q, twin).wait_recv()

    total = b_x_gather[0] + b_x_gather[1] + b_x_gather[2] + b_x_gather[3]
    exact = lax.Precision.HIGHEST
    more_up = dot(total[:, 192:256], router_pad[s], (0, 0), exact)
    more_down = dot(up_router, total[:, 0:192], (1, 0), exact)
    for k in range(4):
        for j in range(4):
            first = 32 * k + 8 * j
            block = a_x_gather[j, 8 * k : 8 * k + 8, 0:192]
            if k < 2:
                up_out[first : first + 8, :] = ADAPTER_SCALE * (block + more_up[first : first + 8])
            else:
                first = first - RANK
                down_out[first : first + 8, :] = block + ADAPTER_SCALE * more_down[first : first + 8]

    sent_over_z(b_z_out, first_b)
    token_copy.wait()


def finish_kernel(*refs):
    sources, targets, held, done = refs[:4], refs[4:8], refs[8:12], refs[12]
    loads = [pltpu.make_async_copy(sources[i], held[i], done.at[0, i]) for i in range(4)]
    stores = [pltpu.make_async_copy(held[i], targets[i], done.at[1, i]) for i in range(4)]
    for one in loads:
        one.start()
    for load, store in zip(loads, stores):
        load.wait()
        store.start()
    for one in stores:
        one.wait()


def per_device(og, scores, idx, router, codes, scales, stored, ctx, down, up):
    vmem = pl.BlockSpec(memory_space=pltpu.VMEM)
    anywhere = pl.BlockSpec(memory_space=pl.ANY)
    shape = jax.ShapeDtypeStruct
    results = (
        shape((256, 1024), BF16),
        shape((128, FEATURES), BF16),
        shape((RANK, 192), F32),
        shape((RANK, 192), F32),
    )
    made = pl.pallas_call(
        layer_kernel,
        out_shape=results,
        in_specs=[anywhere] * 10,
        out_specs=(anywhere, anywhere, vmem, vmem),
        scratch_shapes=[
            pltpu.VMEM((128, FEATURES), BF16),
            pltpu.VMEM((8, 128), F32),
            pltpu.VMEM((2, 128), jnp.int32),
            pltpu.VMEM((8, FEATURES), BF16),
            pltpu.VMEM((192, 256), BF16),
            pltpu.VMEM((3, 1024), BF16),
            pltpu.VMEM((256, 1024), BF16),
            pltpu.VMEM((128, FEATURES), BF16),
            pltpu.VMEM((RANK, FEATURES), BF16),
            pltpu.VMEM((RANK, FEATURES), BF16),
            pltpu.VMEM((4, 4, SLOTS, FEATURES + TAIL), BF16),
            pltpu.VMEM((2, FEATURES, 256), BF16),
            pltpu.VMEM((2, 4, 128, 256), BF16),
            pltpu.VMEM((4, 2, 128, 256), BF16),
            pltpu.VMEM((256, 1024), BF16),
            pltpu.VMEM((128, FEATURES), BF16),
            pltpu.VMEM((256, 128), F32),
            pltpu.VMEM((8, 32, 128), F32),
            pltpu.VMEM((128, FEATURES), F32),
            pltpu.VMEM((128, FEATURES // 2), F32),
            pltpu.VMEM((128, FEATURES // 2), BF16),
            pltpu.VMEM((3, 32, FEATURES // 2), BF16),
            pltpu.VMEM((32, FEATURES // 2), F32),
            pltpu.VMEM((3, 8, FEATURES // 2), F32),
            pltpu.VMEM((8, 8, 256), F32),
            pltpu.VMEM((16, 8, 256), F32),
            pltpu.VMEM((16, 8, 256), F32),
            pltpu.VMEM((8, 8, 256), F32),
            pltpu.VMEM((8, 8, 256), F32),
            pltpu.VMEM((16, 8, 256), F32),
            pltpu.VMEM((4, 8, 256), F32),
            pltpu.VMEM((4, 32, 256), F32),
            pltpu.VMEM((4, 8, 256), F32),
            pltpu.VMEM((4, 8, 256), F32),
            pltpu.VMEM((16, 8, 192), F32),
            pltpu.VMEM((4, SLOTS, TAIL), BF16),
            pltpu.SemaphoreType.DMA((SENDS,)),
            pltpu.SemaphoreType.DMA((RECVS,)),
            pltpu.SemaphoreType.DMA((12,)),
        ],
        compiler_params=pltpu.CompilerParams(
            collective_id=0, has_side_effects=True, vmem_limit_bytes=62 << 20
        ),
    )(og, scores.T, idx.T, router, codes, scales, stored[0, 0], ctx, down, up)
    hidden_grad, token_grad, up_gradient, grad_down = pl.pallas_call(
        finish_kernel,
        out_shape=results,
        in_specs=[anywhere] * 4,
        out_specs=(anywhere,) * 4,
        scratch_shapes=[pltpu.VMEM(one.shape, one.dtype) for one in results]
        + [pltpu.SemaphoreType.DMA((2, 4))],
        compiler_params=pltpu.CompilerParams(vmem_limit_bytes=62 << 20),
    )(*made)
    return hidden_grad.reshape(stored.shape), token_grad, grad_down, up_gradient


def solution(mesh):
    tokens = P(("dp", "expert", "shard"), None)
    blocks = P("shard", "expert")
    hidden = P("dp", "shard", None, "expert")
    shares = P(None, "shard")
    return jax.shard_map(
        per_device,
        mesh=mesh,
        in_specs=(tokens, tokens, tokens, P(), blocks, blocks, hidden, tokens, P(), P()),
        out_specs=(hidden, tokens, shares, shares),
        check_vma=False,
    )
```

```python
import jax
import jax.numpy as jnp
from jax import lax
from jax.experimental import pallas as pl
from jax.experimental.pallas import tpu as pltpu
from jax.sharding import PartitionSpec as P

ADAPTER_SCALE = 0.25
MESH = pl.DeviceIdType.MESH
F32, BF16 = jnp.float32, jnp.bfloat16
FEATURES, TAIL, SLOTS, RANK = 3072, 128, 32, 64
SENDS, RECVS = 120, 140


def dot(a, b, over, precision=None):
    return lax.dot_general(
        a, b, ((over[:1], over[1:]), ((), ())), precision=precision, preferred_element_type=F32
    )


def layer_kernel(
    og_in,
    scores_in,
    idx_in,
    router_in,
    codes_in,
    scales_in,
    stored_in,
    ctx_in,
    down_in,
    up_in,
    hidden_out,
    token_out,
    up_out,
    down_out,
    og,
    scores,
    idx,
    router,
    codes,
    scales,
    stored,
    ctx,
    down,
    up,
    rows,
    weight,
    prod_out,
    prod_in,
    hidden,
    token,
    pg_out,
    pg_in,
    adapt,
    a_twin,
    a_y_out,
    a_y_in,
    a_x_out,
    a_x_in,
    a_z_out,
    a_z_in,
    b_pad,
    b_twin,
    b_z_out,
    b_z_in,
    a_y_gather,
    a_x_gather,
    b_y_gather,
    b_x_gather,
    router_pad,
    twin_probs,
    send,
    recv,
    local,
):
    d, e, s = lax.axis_index("dp"), lax.axis_index("expert"), lax.axis_index("shard")
    y, c = e // 2, e % 2
    twin = (d, y * 2 + 1 - c, s)
    keeps = s // 8 == c

    barrier = pltpu.get_barrier_semaphore()
    for target in (
        twin,
        ((d + 1) % 4, e, s),
        ((d + 3) % 4, e, s),
        (d, (e + 2) % 8, s),
        (d, (e + 6) % 8, s),
        (d, y * 2, (s + 1) % 16),
        (d, y * 2 + 1, (s + 1) % 16),
        (d, y * 2, (s + 15) % 16),
        (d, y * 2 + 1, (s + 15) % 16),
    ):
        pl.semaphore_signal(barrier, inc=1, device_id=target, device_id_type=MESH)

    loads = []
    for i, (src, dst) in enumerate(
        (
            (codes_in.at[:, pl.ds(pl.multiple_of(d * 256, 256), 256)], codes),
            (scales_in, scales),
            (idx_in, idx),
            (scores_in, scores),
            (og_in, og),
            (ctx_in, ctx),
            (down_in, down),
            (up_in, up),
            (stored_in, stored),
            (router_in, router),
        )
    ):
        loads.append(pltpu.make_async_copy(src, dst, local.at[2 + i]))
        loads[-1].start()

    made = []
    used = [0, 0]

    def describe(src, dst, i, j, target):
        return pltpu.make_async_remote_copy(
            src_ref=src,
            dst_ref=dst,
            send_sem=send.at[i],
            recv_sem=recv.at[j],
            device_id=target,
            device_id_type=MESH,
        )

    def start(src, dst, target):
        one = describe(src, dst, used[0], used[1], target)
        used[0] += 1
        used[1] += 1
        one.start()
        made.append(one)
        return one

    def row_range(first, count, step):
        return pl.ds(pl.multiple_of(first, step), count)

    quarter = pl.ds(pl.multiple_of(d * 256, 256), 256)
    loads[0].wait()
    loads[1].wait()
    factors = scales[:, quarter].astype(F32)
    for k in range(3):
        block = codes[64 * k : 64 * k + 64, :].astype(F32) * factors[k : k + 1, :]
        weight[c, row_range(s * 192 + 64 * k, 64, 64), :] = block.astype(BF16)

    f = d * (1 - c) + y * c
    g = y * (1 - c) + d * c

    def at_fg(ff, gg):
        return (ff * (1 - c) + gg * c, gg * (1 - c) + ff * c)

    def device_fg(ff, gg):
        dd, yy = at_fg(ff % 4, gg % 4)
        return (dd, yy * 2 + c, s)

    f_plus, f_minus = device_fg(f + 1, g), device_fg(f + 3, g)
    g_plus, g_minus = device_fg(f, g + 1), device_fg(f, g + 3)
    z_plus = (d, e, (s + 1) % 16)

    def pass_rows(ff, gg, target, part=None):
        dd, yy = at_fg(ff % 4, gg % 4)
        piece = rows.at[dd, yy]
        if part is not None:
            piece = rows.at[dd, yy, pl.ds(16 * part, 16)]
        return start(piece, piece, target)

    def weight_piece(core, owner, part):
        return weight.at[core, row_range((owner % 16) * 192 + 96 * part, 96, 16)]

    turn = 1 - 2 * c
    onward = (d, e, (s + 16 + turn) % 16)
    pl.semaphore_wait(barrier, 9)
    own_up, own_down = [], []
    for part in range(2):
        for core, step, made_first in ((0, 1, own_up), (1, 15, own_down)):
            made_first.append(tuple(used))
            used[0] += 1
            used[1] += 2
            piece = weight_piece(c, s, part)
            describe(
                piece,
                piece,
                made_first[-1][0],
                made_first[-1][1] + c,
                (d, y * 2 + core, (s + step) % 16),
            ).start()
    piece = weight.at[c, row_range(s * 192, 192, 64)]
    weights_to_twin = [start(piece, piece, twin)]
    passing = {}

    def ring_step(h):
        owner = s + 16 - turn * h
        arrived = dict(passing)
        passing.clear()
        for part in range(2):
            for core in range(2):
                if h == 1:
                    first = own_up[part][1] * (1 - c) + own_down[part][1] * c + core
                    piece = weight_piece(core, owner, part)
                    describe(piece, piece, 0, first, twin).wait_recv()
                elif (core, part) in arrived:
                    arrived[core, part].wait_recv()
                if h < 7:
                    piece = weight_piece(core, owner, part)
                    passing[core, part] = start(piece, piece, onward)
                elif h == 7 and core == 1:
                    piece = weight_piece(c, owner, part)
                    passing[core, part] = start(piece, piece, onward)
        rows_of_owner = row_range((owner % 16) * 192, 192, 64)
        piece = weight.at[:, rows_of_owner] if h < 8 else weight.at[c, rows_of_owner]
        weights_to_twin.append(start(piece, piece, twin))

    loads[2].wait()
    loads[3].wait()
    labels = lax.broadcasted_iota(jnp.int32, (8, 128), 0)
    first_choice, second_choice = idx[0:1, :], idx[1:2, :]
    choose_first, choose_second = labels == first_choice, labels == second_choice
    score = scores[...]
    chosen_first = jnp.sum(jnp.where(choose_first, score, 0.0), axis=0, keepdims=True)
    chosen_second = jnp.sum(jnp.where(choose_second, score, 0.0), axis=0, keepdims=True)
    first_prob = 1.0 / (1.0 + jnp.exp(chosen_second - chosen_first))
    second_prob = 1.0 - first_prob
    in_first = (first_choice == 0).astype(F32)
    in_second = (second_choice == 0).astype(F32)
    flag = in_first + in_second
    before = lax.broadcasted_iota(jnp.int32, (128, 128), 0) < lax.broadcasted_iota(
        jnp.int32, (128, 128), 1
    )
    slot = dot(
        jnp.broadcast_to(flag, (16, 128)).astype(BF16),
        jnp.where(before, 1.0, 0.0).astype(BF16),
        (1, 0),
    )[0:1, :]
    slot_labels = lax.broadcasted_iota(jnp.int32, (SLOTS, 128), 0).astype(F32)
    placement = jnp.where(slot == slot_labels, flag, 0.0)
    window_prob = jnp.where(in_first > 0.0, first_prob, second_prob).astype(BF16).astype(F32)

    loads[4].wait()
    rows[d, y, :, 0:FEATURES] = dot(placement.astype(BF16), og[...], (1, 0)).astype(BF16)
    rows[d, y, :, FEATURES : FEATURES + TAIL] = jnp.broadcast_to(
        jnp.sum(placement * window_prob, axis=1, keepdims=True), (SLOTS, TAIL)
    ).astype(BF16)
    to_f_plus = pass_rows(f, g, f_plus)
    to_f_minus = pass_rows(f, g, f_minus)
    g_up, g_down, g_up_half, g_down_half = [], [], [], []

    def spread_g(ff):
        g_up.append(pass_rows(ff, g, g_plus))
        g_down.append(pass_rows(ff, g, g_minus))

    spread_g(f)

    for one in loads[5:]:
        one.wait()
    low_in = dot(ctx[...], down[...], (1, 1)).astype(BF16)
    low_grad = (ADAPTER_SCALE * dot(og[...], up[...], (1, 1))).astype(BF16)

    from_f = (f, f + 3, f + 1, f + 2)

    def take_g(i):
        g_up[i].wait_recv()
        g_up_half.append(pass_rows(from_f[i], g + 3, g_plus, 0))
        g_down[i].wait_recv()
        g_down_half.append(pass_rows(from_f[i], g + 1, g_minus, 1))

    def take_g_half(i):
        g_up_half[i].wait_recv()
        g_down_half[i].wait_recv()

    ring_step(1)
    adapt[0:RANK, :] = dot(low_in, og[...], (0, 0))
    to_f_plus.wait_recv()
    f_up_half = pass_rows(f + 3, g, f_plus, 0)
    spread_g(f + 3)
    to_f_minus.wait_recv()
    f_down_half = pass_rows(f + 1, g, f_minus, 1)
    spread_g(f + 1)
    ring_step(2)
    adapt[RANK : 2 * RANK, :] = dot(low_grad, ctx[...], (0, 0))
    half = FEATURES // 2
    to_twin_a = start(
        adapt.at[:, pl.ds(pl.multiple_of((1 - c) * half, half), half)], a_twin, twin
    )
    take_g(0)
    ring_step(3)
    f_up_half.wait_recv()
    f_down_half.wait_recv()
    spread_g(f + 2)
    ring_step(4)
    take_g_half(0)
    probs_to_twin = start(rows.at[d, :, :, pl.ds(FEATURES, TAIL)], twin_probs, twin)

    to_twin_a.wait_recv()
    a_twin[...] += adapt[:, pl.ds(pl.multiple_of(c * half, half), half)]
    a_y_out[...] = a_twin[...].astype(BF16)
    a_y = []
    for j in range(1, 4):
        to = (y + j) % 4
        a_y.append(
            start(a_y_out.at[row_range(to * 32, 32, 32)], a_y_in.at[j - 1], (d, to * 2 + c, s))
        )

    ring_step(5)
    take_g(1)
    ring_step(6)
    take_g(2)
    ring_step(7)
    take_g_half(1)

    for one in a_y:
        one.wait_recv()
    a_x_out[...] = a_twin[row_range(y * 32, 32, 32), :]
    for j in range(3):
        a_x_out[...] += a_y_in[j].astype(F32)
    a_x = []
    for j in range(1, 4):
        to = (d + j) % 4
        a_x.append(start(a_x_out.at[row_range(to * 8, 8, 8)], a_x_in.at[j - 1], (to, e, s)))

    ring_step(8)
    take_g(3)
    take_g_half(2)
    take_g_half(3)
    for one in weights_to_twin:
        one.wait_recv()

    exchange = []
    for pair in ((2, 1), (3, 0)):
        left = jnp.concatenate(
            [rows[(d + j) % 4, :, :, 0:FEATURES].reshape(128, FEATURES) for j in pair], axis=0
        )
        for k in range(2):
            core = (c + 1 + k) % 2
            product = dot(left, weight[core], (1, 0)).astype(BF16)
            for n, j in enumerate(pair):
                to = (d + j) % 4
                block = product[128 * n : 128 * n + 128]
                if j == 0 and k == 1:
                    prod_in[d, c] = block
                else:
                    prod_out[k, to] = block
                    exchange.append(
                        (j, k, start(prod_out.at[k, to], prod_in.at[d, c], (to, y * 2 + core, s)))
                    )

    for one in a_x:
        one.wait_recv()
    part = a_x_out[row_range(d * 8, 8, 8), :] + a_x_in[0] + a_x_in[1] + a_x_in[2]
    for j in range(8):
        a_z_out[j, :, 0:192] = part[:, 192 * j : 192 * j + 192]
    a_z_out[:, :, 192:256] = jnp.zeros((8, 8, 64), F32)

    def over_z(out, landing):
        first_send, first_recv = used
        used[0] += 8
        used[1] += 16
        for j in range(8):
            k = c * 8 + j

            @pl.when(k != s)
            def _():
                describe(
                    out.at[j], landing.at[s], first_send + j, first_recv + s, (d, e, k)
                ).start()

        return first_send, first_recv

    def sum_over_z(out, landing, first):
        landing[s] = out[s % 8]
        for i in range(16):

            @pl.when(i != s)
            def _():
                describe(out.at[0], landing.at[i], first[0], first[1] + i, z_plus).wait_recv()

        total = landing[0]
        for i in range(1, 16):
            total = total + landing[i]
        return total

    def sent_over_z(out, first):
        for j in range(8):

            @pl.when(c * 8 + j != s)
            def _():
                describe(out.at[j], out.at[j], first[0] + j, first[1], z_plus).wait_send()

    first_a = over_z(a_z_out, a_z_in)

    probs_to_twin.wait_recv()

    def take_product(q, same, first):
        core = c if same else 1 - c
        for k in range(4):
            place = pl.ds(pl.multiple_of(64 * k + 32 * core, 32), SLOTS)
            prob = rows[d, k, :, FEATURES : FEATURES + TAIL] if same else twin_probs[k]
            prob = prob.astype(F32)
            total = None
            for n in range(2):
                columns = pl.ds(pl.multiple_of(q * 256 + 128 * n, 128), 128)
                piece = prod_in[q, core, 32 * k : 32 * k + 32, 128 * n : 128 * n + 128].astype(F32)
                hidden[place, columns] = (prob * piece).astype(BF16)
                term = stored[place, columns].astype(F32) * piece
                total = term if total is None else total + term
            if first:
                pg_out[place, :] = total
            else:
                pg_out[place, :] += total

    take_product(d, True, True)
    order = {(1, 0): 0, (1, 1): 1, (2, 0): 2, (2, 1): 3, (0, 0): 4, (3, 0): 5, (3, 1): 6}
    for j, k, one in sorted(exchange, key=lambda item: order[item[:2]]):
        one.wait_recv()
        take_product((d + 4 - j) % 4, k == 1, (j, k) == (1, 0))
    hidden_copy = pltpu.make_async_copy(hidden, hidden_out, local.at[0])
    hidden_copy.start()

    pg = []
    for p in (4, 5, 3, 2, 6, 7, 1):
        to = (e + p) % 8
        pg.append(start(pg_out.at[row_range(to * 32, 32, 32)], pg_in.at[e], (d, to, s)))
    pg_in[e] = pg_out[row_range(e * 32, 32, 32), :]

    def reserve(sends, recvs):
        first = tuple(used)
        used[0] += sends
        used[1] += recvs
        return first

    def along(buffer, first, axis):
        mine, copies = (y if axis == "y" else d), []
        for j in range(1, 4):
            to = (d, ((y + j) % 4) * 2 + c, s) if axis == "y" else ((d + j) % 4, e, s)
            piece = buffer.at[mine]
            copies.append(describe(piece, piece, first[0] + j - 1, first[1] + j - 1, to))
        return copies

    sems_a_y, sems_a_x, sems_a_twin = reserve(3, 3), reserve(3, 3), reserve(1, 1)
    sems_b_y, sems_b_x = reserve(3, 3), reserve(7, 4)

    @pl.when(keeps)
    def _():
        a_y_gather[y] = sum_over_z(a_z_out, a_z_in, first_a)
        for one in along(a_y_gather, sems_a_y, "y"):
            one.start()

    for one in pg:
        one.wait_recv()
    returned = pg_in[0]
    for k in range(1, 8):
        returned = returned + pg_in[k]
    returned = jnp.sum(returned, axis=1, keepdims=True)
    window_grad = jnp.sum(placement * returned, axis=0, keepdims=True)
    spread = first_prob * second_prob * (window_grad * in_first - window_grad * in_second)
    sign = choose_first.astype(F32) - choose_second.astype(F32)
    logit_grad = (spread * sign).astype(BF16)

    by_feature = dot(logit_grad, ctx[...], (1, 0))
    by_rank = dot(logit_grad, low_in, (1, 0))
    for k in range(16):
        b_pad[k, :, 0:192] = by_feature[:, 192 * k : 192 * k + 192]
        b_pad[k, :, 192:256] = by_rank
    to_twin_b = start(b_pad.at[row_range((1 - c) * 8, 8, 8)], b_twin, twin)
    token[...] = dot(logit_grad, router[...], (0, 0)).astype(BF16)
    token_copy = pltpu.make_async_copy(token, token_out, local.at[1])
    token_copy.start()
    to_twin_b.wait_recv()
    b_z_out[...] = b_pad[row_range(c * 8, 8, 8)] + b_twin[...]
    first_b = over_z(b_z_out, b_z_in)

    a_across = describe(a_x_gather, a_x_gather, sems_a_twin[0], sems_a_twin[1], twin)

    @pl.when(keeps)
    def _():
        for one in along(a_y_gather, sems_a_y, "y"):
            one.wait()
        for k in range(4):
            a_x_gather[d, 8 * k : 8 * k + 8, :] = a_y_gather[k]
        copies = along(a_x_gather, sems_a_x, "x")
        for one in copies:
            one.start()

    for k in range(16):
        router_pad[k] = router[:, 192 * k : 192 * k + 192].astype(F32)
    up_router = dot(up[...], router[...], (1, 1))

    for made_first in own_up + own_down:
        piece = weight_piece(c, s, 0)
        describe(piece, piece, made_first[0], 0, twin).wait_send()
    for one in made:
        one.wait_send()
    sent_over_z(a_z_out, first_a)
    hidden_copy.wait()

    @pl.when(keeps)
    def _():
        for one in along(a_x_gather, sems_a_x, "x"):
            one.wait()
        a_across.start()
        b_y_gather[y] = sum_over_z(b_z_out, b_z_in, first_b)
        by_y = along(b_y_gather, sems_b_y, "y")
        for one in by_y:
            one.start()
        for one in by_y:
            one.wait_recv()
        b_x_gather[d] = b_y_gather[0] + b_y_gather[1] + b_y_gather[2] + b_y_gather[3]
        piece = b_x_gather.at[d]
        by_x = []
        for j in (2, 1, 3, 0):
            for core in (c, 1 - c):
                if j == 0 and core is c:
                    continue
                target = ((d + j) % 4, y * 2 + core, s)
                by_x.append(
                    describe(piece, piece, sems_b_x[0] + len(by_x), sems_b_x[1] + d, target)
                )
        for one in by_x:
            one.start()
        for q in range(4):

            @pl.when(q != d)
            def _():
                slot = b_x_gather.at[q]
                describe(slot, slot, sems_b_x[0], sems_b_x[1] + q, twin).wait_recv()

        for one in by_x + by_y:
            one.wait_send()
        a_across.wait_send()

    @pl.when(jnp.logical_not(keeps))
    def _():
        a_across.wait_recv()
        for q in range(4):
            slot = b_x_gather.at[q]
            describe(slot, slot, sems_b_x[0], sems_b_x[1] + q, twin).wait_recv()

    total = b_x_gather[0] + b_x_gather[1] + b_x_gather[2] + b_x_gather[3]
    exact = lax.Precision.HIGHEST
    more_up = dot(total[:, 192:256], router_pad[s], (0, 0), exact)
    more_down = dot(up_router, total[:, 0:192], (1, 0), exact)
    for k in range(4):
        for j in range(4):
            first = 32 * k + 8 * j
            block = a_x_gather[j, 8 * k : 8 * k + 8, 0:192]
            if k < 2:
                up_out[first : first + 8, :] = ADAPTER_SCALE * (block + more_up[first : first + 8])
            else:
                first = first - RANK
                down_out[first : first + 8, :] = block + ADAPTER_SCALE * more_down[first : first + 8]

    sent_over_z(b_z_out, first_b)
    token_copy.wait()


def finish_kernel(*refs):
    sources, targets, held, done = refs[:4], refs[4:8], refs[8:12], refs[12]
    loads = [pltpu.make_async_copy(sources[i], held[i], done.at[0, i]) for i in range(4)]
    stores = [pltpu.make_async_copy(held[i], targets[i], done.at[1, i]) for i in range(4)]
    for one in loads:
        one.start()
    for load, store in zip(loads, stores):
        load.wait()
        store.start()
    for one in stores:
        one.wait()


def per_device(og, scores, idx, router, codes, scales, stored, ctx, down, up):
    vmem = pl.BlockSpec(memory_space=pltpu.VMEM)
    anywhere = pl.BlockSpec(memory_space=pl.ANY)
    shape = jax.ShapeDtypeStruct
    results = (
        shape((256, 1024), BF16),
        shape((128, FEATURES), BF16),
        shape((RANK, 192), F32),
        shape((RANK, 192), F32),
    )
    made = pl.pallas_call(
        layer_kernel,
        out_shape=results,
        in_specs=[anywhere] * 10,
        out_specs=(anywhere, anywhere, vmem, vmem),
        scratch_shapes=[
            pltpu.VMEM((128, FEATURES), BF16),
            pltpu.VMEM((8, 128), F32),
            pltpu.VMEM((2, 128), jnp.int32),
            pltpu.VMEM((8, FEATURES), BF16),
            pltpu.VMEM((192, 256), BF16),
            pltpu.VMEM((3, 1024), BF16),
            pltpu.VMEM((256, 1024), BF16),
            pltpu.VMEM((128, FEATURES), BF16),
            pltpu.VMEM((RANK, FEATURES), BF16),
            pltpu.VMEM((RANK, FEATURES), BF16),
            pltpu.VMEM((4, 4, SLOTS, FEATURES + TAIL), BF16),
            pltpu.VMEM((2, FEATURES, 256), BF16),
            pltpu.VMEM((2, 4, 128, 256), BF16),
            pltpu.VMEM((4, 2, 128, 256), BF16),
            pltpu.VMEM((256, 1024), BF16),
            pltpu.VMEM((128, FEATURES), BF16),
            pltpu.VMEM((256, 128), F32),
            pltpu.VMEM((8, 32, 128), F32),
            pltpu.VMEM((128, FEATURES), F32),
            pltpu.VMEM((128, FEATURES // 2), F32),
            pltpu.VMEM((128, FEATURES // 2), BF16),
            pltpu.VMEM((3, 32, FEATURES // 2), BF16),
            pltpu.VMEM((32, FEATURES // 2), F32),
            pltpu.VMEM((3, 8, FEATURES // 2), F32),
            pltpu.VMEM((8, 8, 256), F32),
            pltpu.VMEM((16, 8, 256), F32),
            pltpu.VMEM((16, 8, 256), F32),
            pltpu.VMEM((8, 8, 256), F32),
            pltpu.VMEM((8, 8, 256), F32),
            pltpu.VMEM((16, 8, 256), F32),
            pltpu.VMEM((4, 8, 256), F32),
            pltpu.VMEM((4, 32, 256), F32),
            pltpu.VMEM((4, 8, 256), F32),
            pltpu.VMEM((4, 8, 256), F32),
            pltpu.VMEM((16, 8, 192), F32),
            pltpu.VMEM((4, SLOTS, TAIL), BF16),
            pltpu.SemaphoreType.DMA((SENDS,)),
            pltpu.SemaphoreType.DMA((RECVS,)),
            pltpu.SemaphoreType.DMA((12,)),
        ],
        compiler_params=pltpu.CompilerParams(
            collective_id=0, has_side_effects=True, vmem_limit_bytes=62 << 20
        ),
    )(og, scores.T, idx.T, router, codes, scales, stored[0, 0], ctx, down, up)
    hidden_grad, token_grad, up_gradient, grad_down = pl.pallas_call(
        finish_kernel,
        out_shape=results,
        in_specs=[anywhere] * 4,
        out_specs=(anywhere,) * 4,
        scratch_shapes=[pltpu.VMEM(one.shape, one.dtype) for one in results]
        + [pltpu.SemaphoreType.DMA((2, 4))],
        compiler_params=pltpu.CompilerParams(vmem_limit_bytes=62 << 20),
    )(*made)
    return hidden_grad.reshape(stored.shape), token_grad, grad_down, up_gradient


def solution(mesh):
    tokens = P(("dp", "expert", "shard"), None)
    blocks = P("shard", "expert")
    hidden = P("dp", "shard", None, "expert")
    shares = P(None, "shard")
    return jax.shard_map(
        per_device,
        mesh=mesh,
        in_specs=(tokens, tokens, tokens, P(), blocks, blocks, hidden, tokens, P(), P()),
        out_specs=(hidden, tokens, shares, shares),
        check_vma=False,
    )
```
